256 devices in a mesh: replica: 16 (over x, z_lo), dp: 16 (over z_hi, y, core).
Axes of the slice: x: 4, y: 4, z: 8 (z_hi: 2, z_lo: 4; z = z_hi * 4 + z_lo), core: 2. Of those that a mesh axis runs over, the one named last changes fastest.
Arguments:
- tokens: bfloat16 [65536, 8192], P(('replica', 'dp')), may hold values from -6 to 6
- norm_gain: float32 [16, 8192], P('replica'), may hold values from 0.1 to 1.9
- key_weight: bfloat16 [16, 8192, 512], P('replica', 'dp'), may hold values from -0.0625 to 0.0625
- key_cotangent: bfloat16 [65536, 512], P(('replica', 'dp')), may hold values from -6 to 6
- quantized: int32 [16, 8192, 512], P('replica', 'dp'), may hold values from -127 to 127
- scale_exponent: int32 [16, 8192, 4], P('replica', 'dp'), may hold values from -7 to -5
- momentum: float32 [8192, 512], P('dp'), may hold values from -6 to 6
- outer_params: float32 [8192, 512], P('dp'), may hold values from -6 to 6
Outputs:
- keys: bfloat16 [65536, 512], P(('replica', 'dp'))
- token_grad: bfloat16 [65536, 8192], P(('replica', 'dp'))
- weight_grad: bfloat16 [16, 8192, 512], P('replica', 'dp')
- gain_grad: bfloat16 [16, 8192], P('replica', 'dp')
- new_momentum: float32 [8192, 512], P('dp')
- new_params: float32 [8192, 512], P('dp')
The draws below stay inside these ranges and needn't reach their ends.
All inputs are finite; a program needn't handle non-finite values.
Results may differ from the reference program's by a relative error of at most 0.019.
Values may be sent and summed in bfloat16 or wider, within the bound.
No kernel may reach another device: no remote copies, remote signals or barrier semaphores. Data moves between devices by JAX's collectives and lax.ppermute only.
A program may use at most 128 MiB of HBM per device.

```python
import jax
import jax.numpy as jnp
from jax import lax

D = 8192
KVD = 512
FCOL = 512
QBLOCK = 128
TOK_DEV = 256
TOKENS = 65536
N_REPLICA = 16
N_DP = 16


def with_ends(drawn, key, low, largest):
    dims = drawn.shape
    place = [jax.random.randint(jax.random.fold_in(key, axis), (), 0, dims[axis]) for axis in range(len(dims))]
    drawn = drawn.at[tuple(place)].set(low)
    longest = dims.index(max(dims))
    place[longest] = (place[longest] + 1) % dims[longest]
    return drawn.at[tuple(place)].set(largest)


def levels(own_key, shape, split, low, top_value):
    def one(dim, blocks):
        heights = jax.random.uniform(jax.random.fold_in(jax.random.fold_in(own_key, 6), dim), (blocks,), jnp.float32, low / len(split), top_value / len(split))
        return jnp.repeat(jnp.exp(heights), shape[dim] // blocks).reshape((-1,) + (1,) * (len(shape) - dim - 1))

    factor_of = one(*split[0])
    for cut in split[1:]:
        factor_of = factor_of * one(*cut)
    return factor_of


def scatter_about(key, extent, width, most, pieces=(), held_as=jnp.bfloat16):
    values = width * jax.random.normal(key, extent, jnp.float32)
    if pieces:
        values = values * levels(key, extent, pieces, -0.22, 0.18)
    return jnp.clip(values, -most, most).astype(held_as)


def setup_inputs(seed: int = 0) -> dict:
    splits = jax.random.split(jax.random.key(seed), 9)
    return {
        "tokens": scatter_about(splits[0], (TOKENS, D), 1.0, 6.0, ((0, 256),)),
        "norm_gain": jnp.clip(1.0 + 0.18 * jax.random.normal(splits[1], (N_REPLICA, D), jnp.float32), 0.1, 1.9),
        "key_weight": scatter_about(splits[2], (N_REPLICA, D, KVD), D ** -0.5, 0.0625, ((0, 16), (1, 16))),
        "key_cotangent": scatter_about(splits[3], (TOKENS, KVD), 1.0, 6.0, ((0, 256),)),
        "quantized": with_ends(jax.random.randint(splits[4], (N_REPLICA, D, FCOL), -127, 128), jax.random.fold_in(splits[4], 1), -127, 127).astype(jnp.int32),
        "scale_exponent": with_ends(jax.random.randint(splits[5], (N_REPLICA, D, FCOL // QBLOCK), -7, -4), jax.random.fold_in(splits[5], 1), -7, (-4) - 1).astype(jnp.int32),
        "momentum": scatter_about(splits[6], (D, FCOL), 1.0, 6.0, ((0, 16),), jnp.float32),
        "outer_params": scatter_about(splits[7], (D, FCOL), 1.0, 6.0, ((0, 16),), jnp.float32),
    }


epsilon = 1e-05
outer_decay = 0.9
outer_rate = 0.7

def replica_pass(tokens_r, gain_r, weight_r, cotan_r):
    values = tokens_r.astype(jnp.float32)
    inverse_rms = lax.rsqrt(lax.optimization_barrier(jnp.mean(values * values, axis=-1, keepdims=True)) + epsilon)
    normed = values * inverse_rms
    hidden = (normed * gain_r[None, :]).astype(jnp.bfloat16)
    keys = jnp.dot(hidden, weight_r, preferred_element_type=jnp.float32).astype(jnp.bfloat16)
    hidden_grad = lax.dot_general(cotan_r, weight_r, (((1,), (1,)), ((), ())), preferred_element_type=jnp.float32)
    scaled = hidden_grad * gain_r[None, :]
    token_grad = inverse_rms * (scaled - normed * lax.optimization_barrier(jnp.mean(scaled * normed, axis=-1, keepdims=True)))
    groups_hidden = hidden.reshape(N_DP, TOK_DEV, D)
    groups_cotan = cotan_r.reshape(N_DP, TOK_DEV, KVD)
    groups_gain = (hidden_grad * normed).reshape(N_DP, TOK_DEV, D)

    def add_group(carry, items):
        part_hidden, part_cotan, part_gain = items
        term = lax.dot_general(part_hidden, part_cotan, (((0,), (0,)), ((), ())), preferred_element_type=jnp.float32)
        term = term.astype(jnp.bfloat16).astype(jnp.float32)
        gterm = lax.optimization_barrier(jnp.sum(part_gain, axis=0)).astype(jnp.bfloat16).astype(jnp.float32)
        return ((carry[0] + term, carry[1] + gterm), None)
    start = (jnp.zeros((D, KVD), jnp.float32), jnp.zeros((D,), jnp.float32))
    (weight_grad, gain_grad), _ = lax.scan(add_group, start, (groups_hidden, groups_cotan, groups_gain))
    return (keys, token_grad.astype(jnp.bfloat16), weight_grad.astype(jnp.bfloat16), gain_grad.astype(jnp.bfloat16))

def reference(tokens, norm_gain, key_weight, key_cotangent, quantized, scale_exponent, momentum, outer_params):
    per_rep = TOK_DEV * N_DP
    tok_r = tokens.reshape(N_REPLICA, per_rep, D)
    cot_r = key_cotangent.reshape(N_REPLICA, per_rep, KVD)
    keys, token_grad, weight_grad, gain_grad = lax.map(lambda items: replica_pass(*items), (tok_r, norm_gain, key_weight, cot_r))
    scales = jnp.exp2(scale_exponent.astype(jnp.float32))
    blocks = quantized.astype(jnp.float32).reshape(N_REPLICA, D, FCOL // QBLOCK, QBLOCK) * scales[..., None]
    delta = blocks.reshape(N_REPLICA, D, FCOL)
    average = lax.optimization_barrier(jnp.sum(delta, axis=0)) / N_REPLICA
    new_momentum = outer_decay * momentum + average
    new_params = outer_params - outer_rate * (average + outer_decay * new_momentum)
    return (keys.reshape(TOKENS, KVD), token_grad.reshape(TOKENS, D), weight_grad, gain_grad, new_momentum, new_params)
```

```python
import functools

import jax
import jax.numpy as jnp
from jax import lax
from jax.experimental import pallas as pl
from jax.experimental.pallas import tpu as pltpu
from jax.sharding import PartitionSpec as P

epsilon = 1e-05
outer_decay = 0.9
outer_rate = 0.7

F32 = jnp.float32
BF16 = jnp.bfloat16
N_Y, N_ZH, N_CORE = 4, 2, 2
N_X, N_ZL = 4, 4
VMEM_LIMIT = 50 * 1024 * 1024


def dp_moves(dy=0, dz=0, dc=0):
    pairs = []
    for zh in range(N_ZH):
        for y in range(N_Y):
            for c in range(N_CORE):
                to = (((zh + dz) % N_ZH) * N_Y + (y + dy) % N_Y) * N_CORE + (c + dc) % N_CORE
                pairs.append(((zh * N_Y + y) * N_CORE + c, to))
    return pairs


def to_up(v):
    return lax.ppermute(v, "dp", dp_moves(dy=1))


def to_down(v):
    return lax.ppermute(v, "dp", dp_moves(dy=-1))


def to_far(v):
    return lax.ppermute(v, "dp", dp_moves(dz=1))


def to_core(v):
    return lax.ppermute(v, "dp", dp_moves(dc=1))


def along_x(v, dx):
    pairs = [(x * N_ZL + z, ((x + dx) % N_X) * N_ZL + z) for x in range(N_X) for z in range(N_ZL)]
    return lax.ppermute(v, "replica", pairs)


def row_block(other_side, other_core, dy):
    me = lax.axis_index("dp")
    c = lax.rem(me, N_CORE)
    y = lax.rem(lax.div(me, N_CORE), N_Y)
    zh = lax.div(me, N_CORE * N_Y)
    if other_side:
        zh = 1 - zh
    if other_core:
        c = 1 - c
    return (zh * N_Y + lax.rem(y + dy, N_Y)) * N_CORE + c


def call(kernel, outs, ins, flops=0, nbytes=0, **kw):
    return pl.pallas_call(
        kernel,
        out_shape=outs,
        compiler_params=pltpu.CompilerParams(vmem_limit_bytes=VMEM_LIMIT),
        cost_estimate=pl.CostEstimate(flops=flops, bytes_accessed=nbytes, transcendentals=0),
        **kw,
    )(*ins)


def full(shape):
    return pl.BlockSpec(shape, lambda j: (0,) * len(shape))


def dot_tn(a, b):
    return lax.dot_general(a, b, (((0,), (0,)), ((), ())), preferred_element_type=F32)


def dot_nt(a, b):
    return lax.dot_general(a, b, (((1,), (1,)), ((), ())), preferred_element_type=F32)


def first_partials(tokens, gains, cot):
    t, d = tokens.shape
    k = cot.shape[1]
    f = k

    def kernel(tok, gain, ct, out, ir_out):
        j = pl.program_id(0)

        @pl.when(j == 0)
        def _():
            total = jnp.zeros((t, 128), F32)
            for i in range(d // 512):
                v = tok[:, i * 512 : (i + 1) * 512].astype(F32)
                v = v * v
                total += (v[:, :128] + v[:, 128:256]) + (v[:, 256:384] + v[:, 384:])
            mean = jnp.sum(total, axis=1, keepdims=True) / d
            ir_out[...] = jnp.broadcast_to(lax.rsqrt(mean + epsilon), (t, 128))

        cols = pl.ds(pl.multiple_of(row_block(True, True, j + 1) * f, f), f)
        hidden = (tok[:, cols].astype(F32) * ir_out[:, 0:1] * gain[:, cols]).astype(BF16)
        out[...] = dot_tn(hidden, ct[...]).astype(BF16)

    return call(
        kernel,
        (jax.ShapeDtypeStruct((N_Y * f, k), BF16), jax.ShapeDtypeStruct((t, 128), F32)),
        (tokens, gains, cot),
        flops=2 * t * N_Y * f * k,
        nbytes=2 * t * d + 2 * N_Y * f * k,
        grid=(N_Y,),
        in_specs=[full((t, d)), full((1, d)), full((t, k))],
        out_specs=(pl.BlockSpec((f, k), lambda j: (j, 0)), full((t, 128))),
    )


def partner_partials(tokens, gains, cot, ir):
    t, d = tokens.shape
    k = cot.shape[1]
    f = k

    def kernel(tok, gain, ct, irr, out):
        hidden = (tok[...].astype(F32) * irr[:, 0:1] * gain[...]).astype(BF16)
        out[...] = dot_tn(hidden, ct[...]).astype(BF16)

    return call(
        kernel,
        jax.ShapeDtypeStruct((N_Y * f, k), BF16),
        (tokens, gains, cot, ir),
        flops=2 * t * N_Y * f * k,
        nbytes=2 * t * N_Y * f + 2 * N_Y * f * k,
        grid=(N_Y,),
        in_specs=[
            pl.BlockSpec((t, f), lambda j: (0, row_block(False, True, j + 1))),
            pl.BlockSpec((1, f), lambda j: (0, row_block(False, True, j + 1))),
            full((t, k)),
            full((t, 128)),
        ],
        out_specs=pl.BlockSpec((f, k), lambda j: (j, 0)),
    )


def own_partials(tokens, gains, cot, ir, arrived, other_side):
    t, d = tokens.shape
    k = cot.shape[1]
    f = k
    h = f // 2

    def kernel(tok, gain, ct, irr, arr, up, down, up_later, down_later, own):
        j = pl.program_id(0)
        hidden = (tok[...].astype(F32) * irr[:, 0:1] * gain[...]).astype(BF16)
        total = (dot_tn(hidden, ct[...]) + arr[...].astype(F32)).astype(BF16)

        @pl.when(j == 0)
        def _():
            up_later[...] = total[:h]
            up[h:, :] = total[h:]

        @pl.when(j == 1)
        def _():
            up[:h, :] = total[:h]
            down[h:, :] = total[h:]

        @pl.when(j == 2)
        def _():
            down[:h, :] = total[:h]
            down_later[...] = total[h:]

        @pl.when(j == 3)
        def _():
            own[...] = total

    block = jax.ShapeDtypeStruct((f, k), BF16)
    half = jax.ShapeDtypeStruct((h, k), BF16)
    return call(
        kernel,
        (block, block, half, half, block),
        (tokens, gains, cot, ir, arrived),
        flops=2 * t * N_Y * f * k,
        nbytes=2 * t * N_Y * f + 4 * N_Y * f * k,
        grid=(N_Y,),
        in_specs=[
            pl.BlockSpec((t, f), lambda j: (0, row_block(other_side, False, j + 1))),
            pl.BlockSpec((1, f), lambda j: (0, row_block(other_side, False, j + 1))),
            full((t, k)),
            full((t, 128)),
            pl.BlockSpec((f, k), lambda j: (j, 0)),
        ],
        out_specs=(full((f, k)), full((f, k)), full((h, k)), full((h, k)), full((f, k))),
    )


def ring_terms(up, down, up_later, down_later):
    h = up_later.shape[0]
    from_down = to_up(up)
    from_up = to_down(down)
    last_down = to_up(up_later + from_down[:h])
    last_up = to_down(down_later + from_up[h:])
    return from_down, from_up, last_down, last_up


def side_sum(own, from_down, from_up, last_down, last_up):
    f, k = own.shape
    h = f // 2

    def kernel(o, fd, fu, ld, lu, out):
        out[:h, :] = (o[:h].astype(F32) + fu[:h].astype(F32) + ld[...].astype(F32)).astype(BF16)
        out[h:, :] = (o[h:].astype(F32) + fd[h:].astype(F32) + lu[...].astype(F32)).astype(BF16)

    return call(
        kernel,
        jax.ShapeDtypeStruct((f, k), BF16),
        (own, from_down, from_up, last_down, last_up),
        flops=4 * f * k,
        nbytes=10 * f * k,
    )


def final_sum(own, from_down, from_up, last_down, last_up, far, weight, gains):
    f, k = own.shape
    h = f // 2

    def kernel(o, fd, fu, ld, lu, fr, w, gain, out, gain_out):
        top = (o[:h].astype(F32) + fu[:h].astype(F32)) + (ld[...].astype(F32) + fr[:h].astype(F32))
        bottom = (o[h:].astype(F32) + fd[h:].astype(F32)) + (lu[...].astype(F32) + fr[h:].astype(F32))
        out[:h, :] = top.astype(BF16)
        out[h:, :] = bottom.astype(BF16)
        ones = jnp.ones((8, k), F32)
        cols = pl.ds(pl.multiple_of(lax.axis_index("dp") * f, f), f)
        g = gain[:, cols]
        for i, part in enumerate((top, bottom)):
            rows = slice(i * h, (i + 1) * h)
            sums = lax.dot_general(
                ones,
                part * w[rows].astype(F32),
                (((1,), (1,)), ((), ())),
                preferred_element_type=F32,
                precision=lax.Precision.HIGHEST,
            )
            gain_out[:, rows] = (sums[0:1] / g[:, rows]).astype(BF16)

    return call(
        kernel,
        (jax.ShapeDtypeStruct((f, k), BF16), jax.ShapeDtypeStruct((1, f), BF16)),
        (own, from_down, from_up, last_down, last_up, far, weight, gains),
        flops=40 * f * k,
        nbytes=14 * f * k,
    )


def ring_gather(rows):
    h = rows.shape[0] // 2
    from_down = to_up(rows)
    from_up = to_down(rows)
    return rows, from_down, from_up, to_up(from_down[:h]), to_down(from_up[h:])


GATHERED = ((0, 0), (3, 0), (1, 0), (2, 0), (2, 1))


def gathered_columns(other_side, other_core, which, f):
    dy, second = GATHERED[which]
    n = f // 2 if which >= 3 else f
    start = row_block(other_side, other_core, dy) * f + second * (f // 2)
    return pl.ds(pl.multiple_of(start, f // 2), n)


def project(tokens, gains, ir, weights, other_side, before=None, cot=None):
    t, d = tokens.shape
    f, k = weights[0][0].shape
    flat = tuple(weights[0]) + tuple(weights[1])
    n = len(flat)

    def kernel(*refs):
        tok, gain, irr = refs[:3]
        ws = refs[3 : 3 + n]
        rest = refs[3 + n :]
        scale = irr[:, 0:1]
        acc = jnp.zeros((t, k), F32) if before is None else rest[0][...]
        for i, w in enumerate(ws):
            cols = gathered_columns(other_side, i >= n // 2, i % (n // 2), f)
            hidden = (tok[:, cols].astype(F32) * scale * gain[:, cols]).astype(BF16)
            acc += jnp.dot(hidden, w[...], preferred_element_type=F32)
        if before is None:
            rest[0][...] = acc
        else:
            ct, keys, mean = rest[1:]
            keys[...] = acc.astype(BF16)
            row = jnp.sum(acc * ct[...].astype(F32), axis=1, keepdims=True) / d
            mean[...] = jnp.broadcast_to(row, (t, 128))

    ins = (tokens, gains, ir) + flat
    if before is None:
        outs = jax.ShapeDtypeStruct((t, k), F32)
    else:
        ins += (before, cot)
        outs = (jax.ShapeDtypeStruct((t, k), BF16), jax.ShapeDtypeStruct((t, 128), F32))
    return call(kernel, outs, ins, flops=t * d * k, nbytes=t * d * 2 + d * k)


def backward(tokens, gains, ir, mean, cot, own_side, far_side):
    t, d = tokens.shape
    f, k = own_side[0][0].shape
    flat = own_side[0] + own_side[1] + far_side[0] + far_side[1]
    n = len(own_side[0])

    def kernel(*refs):
        tok, gain, irr, mn, ct = refs[:5]
        ws = refs[5:-1]
        out = refs[-1]
        scale = irr[:, 0:1]
        shift = scale * scale * mn[:, 0:1]
        for i, w in enumerate(ws):
            cols = gathered_columns(i >= 2 * n, (i // n) % 2 == 1, i % n, f)
            grad = dot_nt(ct[...], w[...])
            x = tok[:, cols].astype(F32)
            out[:, cols] = (scale * (grad * gain[:, cols]) - x * shift).astype(BF16)

    return call(
        kernel,
        jax.ShapeDtypeStruct((t, d), BF16),
        (tokens, gains, ir, mean, cot) + flat,
        flops=2 * t * d * k,
        nbytes=4 * t * d + 2 * d * k,
    )


def outer_update(average, momentum, outer_params):
    new_momentum = outer_decay * momentum + average
    new_params = outer_params - outer_rate * (average + outer_decay * new_momentum)
    return (new_momentum, new_params)


def replica_sum(delta):
    n_rep = N_X * N_ZL
    x_groups = [[x * N_ZL + z for x in range(N_X)] for z in range(N_ZL)]
    z_groups = [[x * N_ZL + z for z in range(N_ZL)] for x in range(N_X)]
    part = lax.psum_scatter(
        delta, "replica", scatter_dimension=0, tiled=True, axis_index_groups=x_groups
    )
    part = lax.psum(part, "replica", axis_index_groups=z_groups)
    pieces = [part] + [along_x(part, dx) for dx in (1, 2, 3)]
    x = lax.axis_index("replica") // N_ZL
    rows = part.shape[0]
    total = jnp.zeros_like(delta)
    for i, piece in enumerate(pieces):
        total = lax.dynamic_update_slice(total, piece, (((x - i) % N_X) * rows, 0))
    return total


def shards(
    tokens, norm_gain, key_weight, key_cotangent, quantized, scale_exponent, momentum, outer_params
):
    gains = norm_gain
    weight = key_weight[0]

    scales = jnp.exp2(scale_exponent[0].astype(F32))
    frag_rows, frag_cols = quantized.shape[1:]
    blocks = (
        quantized[0].astype(F32).reshape(frag_rows, scales.shape[1], frag_cols // scales.shape[1])
        * scales[..., None]
    )
    delta = blocks.reshape(frag_rows, frag_cols).astype(BF16)
    total = replica_sum(delta).astype(F32)
    new_momentum, new_params = outer_update(total / lax.axis_size("replica"), momentum, outer_params)

    far_weight = to_far(weight)
    own_rows = ring_gather(weight)
    own_swapped = tuple(to_core(v) for v in own_rows)

    partner_far, ir = first_partials(tokens, gains, key_cotangent)
    arrived_far = to_core(partner_far)
    partner_near = partner_partials(tokens, gains, key_cotangent, ir)
    arrived_near = to_core(partner_near)

    packed = own_partials(tokens, gains, key_cotangent, ir, arrived_far, True)
    far_sum = to_far(side_sum(packed[4], *ring_terms(*packed[:4])))

    far_rows = ring_gather(far_weight)
    far_swapped = tuple(to_core(v) for v in far_rows)

    packed = own_partials(tokens, gains, key_cotangent, ir, arrived_near, False)
    terms = ring_terms(*packed[:4])

    near_keys = project(tokens, gains, ir, (own_rows, own_swapped), False)
    keys, mean = project(
        tokens, gains, ir, (far_rows, far_swapped), True, near_keys, key_cotangent
    )
    token_grad = backward(
        tokens, gains, ir, mean, key_cotangent, (own_rows, own_swapped), (far_rows, far_swapped)
    )
    weight_grad, gain_grad = final_sum(packed[4], *terms, far_sum, weight, gains)
    return (keys, token_grad, weight_grad[None], gain_grad, new_momentum, new_params)


def solution(mesh):
    return jax.shard_map(
        shards,
        mesh=mesh,
        in_specs=(
            P(("replica", "dp"), None),
            P("replica", None),
            P("replica", "dp", None),
            P(("replica", "dp"), None),
            P("replica", "dp", None),
            P("replica", "dp", None),
            P("dp", None),
            P("dp", None),
        ),
        out_specs=(
            P(("replica", "dp"), None),
            P(("replica", "dp"), None),
            P("replica", "dp", None),
            P("replica", "dp"),
            P("dp", None),
            P("dp", None),
        ),
        check_vma=False,
    )
```

```python
import jax
import jax.numpy as jnp
from jax import lax
from jax.experimental import pallas as pl
from jax.experimental.pallas import tpu as pltpu
from jax.sharding import PartitionSpec as P

epsilon = 1e-05
outer_decay = 0.9
outer_rate = 0.7

F32 = jnp.float32
BF16 = jnp.bfloat16
N_Y, N_ZH, N_CORE = 4, 2, 2
N_CHIP = N_Y * N_ZH
N_X, N_ZL = 4, 4
WEIGHT = 1e10
VMEM_LIMIT = 40 * 1024 * 1024


def dp_moves(dy=0, dz=0, dc=0):
    pairs = []
    for zh in range(N_ZH):
        for y in range(N_Y):
            for c in range(N_CORE):
                to = (((zh + dz) % N_ZH) * N_Y + (y + dy) % N_Y) * N_CORE + (c + dc) % N_CORE
                pairs.append(((zh * N_Y + y) * N_CORE + c, to))
    return pairs


def to_up(v):
    return lax.ppermute(v, "dp", dp_moves(dy=1))


def to_down(v):
    return lax.ppermute(v, "dp", dp_moves(dy=-1))


def to_far(v):
    return lax.ppermute(v, "dp", dp_moves(dz=1))


def to_core(v):
    return lax.ppermute(v, "dp", dp_moves(dc=1))


def swap_x(v, bit):
    return lax.ppermute(
        v, "replica", [(x * N_ZL + z, (x ^ bit) * N_ZL + z) for x in range(N_X) for z in range(N_ZL)]
    )


def swap_z(v, bit):
    return lax.ppermute(
        v, "replica", [(x * N_ZL + z, x * N_ZL + (z ^ bit)) for x in range(N_X) for z in range(N_ZL)]
    )


def core():
    return lax.rem(lax.axis_index("dp"), N_CORE)


def chip(side, dy):
    mine = lax.div(lax.axis_index("dp"), N_CORE)
    zh = lax.rem(lax.div(mine, N_Y) + side, N_ZH)
    return zh * N_Y + lax.rem(lax.rem(mine, N_Y) + dy, N_Y)


def place(side, dy):
    return chip(side, dy) * N_CORE + core()


def call(kernel, outs, ins, cost=1.0, vmem=VMEM_LIMIT, **kw):
    return pl.pallas_call(
        kernel,
        out_shape=outs,
        compiler_params=pltpu.CompilerParams(vmem_limit_bytes=vmem),
        cost_estimate=pl.CostEstimate(
            flops=int(cost * WEIGHT), bytes_accessed=0, transcendentals=0
        ),
        **kw,
    )(*ins)


HBM = pl.BlockSpec(memory_space=pltpu.HBM)
INSIDE = pl.BlockSpec(memory_space=pltpu.VMEM)


def full(shape):
    return pl.BlockSpec(shape, lambda j: (0,) * len(shape))


def block(index, size):
    return pl.ds(pl.multiple_of(index * size, size), size)


def dot_nt(a, b):
    return lax.dot_general(a, b, (((1,), (1,)), ((), ())), preferred_element_type=F32)


def dot(a, b):
    return jnp.dot(a, b, preferred_element_type=F32)


def identity(n):
    r = lax.broadcasted_iota(jnp.int32, (n, n), 0)
    c = lax.broadcasted_iota(jnp.int32, (n, n), 1)
    return jnp.where(r == c, 1.0, 0.0).astype(BF16)


def start_all(copies):
    for copy in copies:
        copy.start()
    return copies


ORDER = (2, 3, 1, 0)


def split_tokens(tokens, cot):
    t, d = tokens.shape
    f = cot.shape[1]
    steps = d // (2 * f)

    def kernel(tok, ct, sent, extra, ir_out, held, sems, out_sems):
        arrivals = start_all(
            [
                pltpu.make_async_copy(
                    tok.at[:, 2 * f * i : 2 * f * (i + 1)],
                    held.at[:, 2 * f * i : 2 * f * (i + 1)],
                    sems.at[i],
                )
                for i in range(steps)
            ]
        )
        away = 1 - core()
        leaving = []
        acc = jnp.zeros((t, 128), F32)
        for i in range(steps):
            arrivals[i].wait()
            copy = pltpu.make_async_copy(
                held.at[:, block(2 * i + away, f)],
                sent.at[:, i * f : (i + 1) * f],
                out_sems.at[i],
            )
            copy.start()
            leaving.append(copy)
            for n in range(2 * f * i, 2 * f * (i + 1), 128):
                v = held[:, n : n + 128].astype(F32)
                acc += v * v
        mean = jnp.sum(acc, axis=1, keepdims=True) / d
        ir = lax.rsqrt(jnp.broadcast_to(mean, (t, 128)) + epsilon)
        ir_out[...] = ir
        high = ir.astype(BF16).astype(F32)
        middle = (ir - high).astype(BF16).astype(F32)
        low = ir - high - middle
        lane = lax.broadcasted_iota(jnp.int32, (t, 128), 1)
        terms = jnp.where(lane == 0, high, jnp.where(lane == 1, middle, low))
        extra[:, :f] = ct[...]
        extra[:, f:] = terms.astype(BF16)
        for copy in leaving:
            copy.wait()

    return call(
        kernel,
        (
            jax.ShapeDtypeStruct((t, d // 2), BF16),
            jax.ShapeDtypeStruct((t, f + 128), BF16),
            jax.ShapeDtypeStruct((t, 128), F32),
        ),
        (tokens, cot),
        vmem=60 * 1024 * 1024,
        cost=3.2,
        in_specs=[HBM, INSIDE],
        out_specs=(HBM, INSIDE, INSIDE),
        scratch_shapes=[
            pltpu.VMEM((t, d), BF16),
            pltpu.SemaphoreType.DMA((steps,)),
            pltpu.SemaphoreType.DMA((steps,)),
        ],
    )


def partner_scale(extra, f):
    return sum(extra[:, f + i : f + i + 1].astype(F32) for i in range(3))


def partials(tokens, gains, cot, ir, other, extra, side):
    t, d = tokens.shape
    f = k = cot.shape[1]

    def kernel(tok, oth, gain, ct, irr, ext, *refs):
        hid_out, outs = refs[0], refs[1:5]
        xs, ys, hid, grads, cot_t, in_sems, out_sems = refs[5:]
        arrivals = []
        for i, dy in enumerate(ORDER):
            arrivals += start_all(
                [
                    pltpu.make_async_copy(
                        tok.at[:, block(place(side, dy), f)], xs.at[i], in_sems.at[0, i]
                    ),
                    pltpu.make_async_copy(
                        oth.at[:, block(chip(side, dy), f)], ys.at[i], in_sems.at[1, i]
                    ),
                ]
            )
        eye = identity(k)
        cot_t[:, :t] = dot_nt(eye, ct[...]).astype(BF16)
        cot_t[:, t:] = dot_nt(eye, ext[:, :k]).astype(BF16)
        own_scale = irr[:, 0:1]
        other_scale = partner_scale(ext, f)
        leaving = []
        for i, dy in enumerate(ORDER):
            g = gain[:, block(place(side, dy), f)]
            arrivals[2 * i].wait()
            arrivals[2 * i + 1].wait()
            cols = slice(i * f, (i + 1) * f)
            hid[:t, cols] = (xs[i].astype(F32) * own_scale * g).astype(BF16)
            hid[t:, cols] = (ys[i].astype(F32) * other_scale * g).astype(BF16)
            grads[i] = dot(cot_t[...], hid[:, cols]).astype(BF16)
            leaving += start_all(
                [
                    pltpu.make_async_copy(grads.at[i], outs[i], out_sems.at[0, i]),
                    pltpu.make_async_copy(hid.at[:, cols], hid_out.at[:, cols], out_sems.at[1, i]),
                ]
            )
        for copy in leaving:
            copy.wait()

    shape = jax.ShapeDtypeStruct((k, f), BF16)
    return call(
        kernel,
        (jax.ShapeDtypeStruct((2 * t, N_Y * f), BF16),) + (shape,) * 4,
        (tokens, other, gains, cot, ir, extra),
        cost=3.4,
        in_specs=[HBM, HBM] + [INSIDE] * 4,
        out_specs=(HBM,) * 5,
        scratch_shapes=[
            pltpu.VMEM((N_Y, t, f), BF16),
            pltpu.VMEM((N_Y, t, f), BF16),
            pltpu.VMEM((2 * t, N_Y * f), BF16),
            pltpu.VMEM((N_Y, k, f), BF16),
            pltpu.VMEM((k, 2 * t), BF16),
            pltpu.SemaphoreType.DMA((2, N_Y)),
            pltpu.SemaphoreType.DMA((2, N_Y)),
        ],
    )


def side_sum(own, from_down, from_up):
    def kernel(o, a, b, out):
        out[...] = (o[...].astype(F32) + a[...].astype(F32) + b[...].astype(F32)).astype(BF16)

    return call(kernel, jax.ShapeDtypeStruct(own.shape, BF16), (own, from_down, from_up), cost=1.0)


def final_sum(own, from_down, from_up, far, weight, gains):
    k, f = own.shape

    def kernel(o, a, b, fr, w, gain, out, gain_out):
        eye = identity(k)
        weight_t = dot_nt(eye, w[...])
        total = (o[...].astype(F32) + a[...].astype(F32)) + (b[...].astype(F32) + fr[...].astype(F32))
        out[...] = dot_nt(eye, total.astype(BF16)).astype(BF16)
        sums = jnp.sum(total * weight_t, axis=0, keepdims=True)
        gain_out[...] = (sums / gain[:, block(lax.axis_index("dp"), f)]).astype(BF16)

    return call(
        kernel,
        (jax.ShapeDtypeStruct((f, k), BF16), jax.ShapeDtypeStruct((1, f), BF16)),
        (own, from_down, from_up, far, weight, gains),
        cost=2.9,
    )


def project(hidden, weights, before=None, cot=None, extra=None):
    f, k = weights[0].shape
    t = hidden.shape[0] // 2
    last = before is not None

    def kernel(*refs):
        hid, ws = refs[0], refs[1:5]
        held, hs, sems = refs[-3:]
        arrivals = []
        for i in range(N_Y):
            arrivals += start_all(
                [
                    pltpu.make_async_copy(ws[i], held.at[i], sems.at[0, i]),
                    pltpu.make_async_copy(hid.at[:, i * f : (i + 1) * f], hs.at[i], sems.at[1, i]),
                ]
            )
        total = refs[5][...] if last else jnp.zeros((2 * t, k), F32)
        for i in range(N_Y):
            arrivals[2 * i].wait()
            arrivals[2 * i + 1].wait()
            total += dot(hs[i], held[i])
        if not last:
            refs[5][...] = total
            return
        ct, ext, mine, sent = refs[6:10]
        own = jnp.sum(total[:t] * ct[...].astype(F32), axis=1, keepdims=True)
        others = jnp.sum(total[t:] * ext[:, :k].astype(F32), axis=1, keepdims=True)
        lane = lax.broadcasted_iota(jnp.int32, (t, 128), 1)
        mine[:, :k] = total[:t]
        mine[:, k:] = jnp.where(lane == 0, own, others)
        sent[:, :k] = total[t:]
        sent[:, k:] = jnp.where(lane == 0, others, own)

    ins = (hidden,) + tuple(weights)
    specs = [HBM] * 5
    if last:
        ins += (before, cot, extra)
        specs += [INSIDE] * 3
        outs = (jax.ShapeDtypeStruct((t, k + 128), F32),) * 2
        out_specs = (INSIDE,) * 2
    else:
        outs = jax.ShapeDtypeStruct((2 * t, k), F32)
        out_specs = INSIDE
    return call(
        kernel,
        outs,
        ins,
        cost=2.5,
        in_specs=specs,
        out_specs=out_specs,
        scratch_shapes=[
            pltpu.VMEM((N_Y, f, k), BF16),
            pltpu.VMEM((N_Y, 2 * t, f), BF16),
            pltpu.SemaphoreType.DMA((2, N_Y)),
        ],
    )


def blocks_of_chip():
    return [(side, dy) for side in range(N_ZH) for dy in ORDER]


def backward_scratch(t, f, k):
    return [
        pltpu.VMEM((N_CHIP, f, k), BF16),
        pltpu.VMEM((N_CHIP, t, f), BF16),
        pltpu.VMEM((N_CHIP, t, f), BF16),
        pltpu.SemaphoreType.DMA((2, N_CHIP)),
        pltpu.SemaphoreType.DMA((N_CHIP,)),
    ]


def token_gradient(x_from, ws, out_to, gain, ct, scale, mean, scratch):
    held, xs, results, sems, out_sems = scratch
    arrivals = []
    for i, w in enumerate(ws):
        arrivals += start_all(
            [
                pltpu.make_async_copy(w, held.at[i], sems.at[0, i]),
                pltpu.make_async_copy(x_from(i), xs.at[i], sems.at[1, i]),
            ]
        )
    shift = scale * scale * mean
    leaving = []
    for i, (side, dy) in enumerate(blocks_of_chip()):
        arrivals[2 * i].wait()
        arrivals[2 * i + 1].wait()
        g = gain[:, block(place(side, dy), held.shape[1])]
        grad = dot_nt(ct, held[i])
        results[i] = (scale * (grad * g) - xs[i].astype(F32) * shift).astype(BF16)
        leaving += start_all([pltpu.make_async_copy(results.at[i], out_to(i), out_sems.at[i])])
    for copy in leaving:
        copy.wait()


def backward_other(other, extra, gains, mine, arrived, weights):
    t = other.shape[0]
    f = k = extra.shape[1] - 128
    d = gains.shape[1]
    where = blocks_of_chip()

    def kernel(*refs):
        oth, gain, ext, mn, arr = refs[:5]
        ws = refs[5:13]
        out, keys, mean = refs[13:16]
        keys[...] = (mn[:, :k] + arr[:, :k]).astype(BF16)
        means = (mn[:, k:] + arr[:, k:]) / d
        mean[...] = means
        token_gradient(
            lambda i: oth.at[:, block(chip(*where[i]), f)],
            ws,
            lambda i: out.at[:, i * f : (i + 1) * f],
            gain,
            ext[:, :k],
            partner_scale(ext, f),
            means[:, 1:2],
            refs[16:],
        )

    return call(
        kernel,
        (
            jax.ShapeDtypeStruct((t, d // 2), BF16),
            jax.ShapeDtypeStruct((t, k), BF16),
            jax.ShapeDtypeStruct((t, 128), F32),
        ),
        (other, gains, extra, mine, arrived) + tuple(weights),
        cost=5.5,
        in_specs=[HBM] + [INSIDE] * 4 + [HBM] * 8,
        out_specs=(HBM, INSIDE, INSIDE),
        scratch_shapes=backward_scratch(t, f, k),
    )


def backward_own(tokens, gains, ir, cot, mean, weights):
    t, d = tokens.shape
    f = k = cot.shape[1]
    where = blocks_of_chip()

    def kernel(*refs):
        tok, gain, irr, ct, mn = refs[:5]
        ws = refs[5:13]
        out = refs[13]
        token_gradient(
            lambda i: tok.at[:, block(place(*where[i]), f)],
            ws,
            lambda i: out.at[:, block(place(*where[i]), f)],
            gain,
            ct[...],
            irr[:, 0:1],
            mn[:, 0:1],
            refs[14:],
        )

    return call(
        kernel,
        jax.ShapeDtypeStruct((t, d), BF16),
        (tokens, gains, ir, cot, mean) + tuple(weights),
        cost=4.7,
        in_specs=[HBM] + [INSIDE] * 4 + [HBM] * 8,
        out_specs=HBM,
        scratch_shapes=backward_scratch(t, f, k),
    )


def fill_in(token_grad, arrived):
    t = arrived.shape[0]
    f = arrived.shape[1] // N_CHIP
    where = blocks_of_chip()

    def kernel(_, arr, out, held, sems):
        away = 1 - core()
        arrivals = start_all(
            [
                pltpu.make_async_copy(arr.at[:, i * f : (i + 1) * f], held.at[i], sems.at[0, i])
                for i in range(N_CHIP)
            ]
        )
        leaving = []
        for i in range(N_CHIP):
            arrivals[i].wait()
            to = out.at[:, block(chip(*where[i]) * N_CORE + away, f)]
            leaving += start_all([pltpu.make_async_copy(held.at[i], to, sems.at[1, i])])
        for copy in leaving:
            copy.wait()

    return call(
        kernel,
        jax.ShapeDtypeStruct(token_grad.shape, token_grad.dtype),
        (token_grad, arrived),
        cost=1.4,
        in_specs=[HBM, HBM],
        out_specs=HBM,
        input_output_aliases={0: 0},
        scratch_shapes=[
            pltpu.VMEM((N_CHIP, t, f), BF16),
            pltpu.SemaphoreType.DMA((2, N_CHIP)),
        ],
    )


def x_bit(bit):
    return lax.rem(lax.div(lax.axis_index("replica"), N_ZL * bit), 2)


def scaled_halves(quantized, exponents):
    n, cols = quantized.shape
    h = n // 2
    nb = exponents.shape[1]
    width = cols // nb

    def kernel(q, e, keep, send):
        for out, half in ((keep, x_bit(1)), (send, 1 - x_bit(1))):
            rows = pl.ds(pl.multiple_of(half * h, h), h)
            scale = jnp.exp2(e[rows, :].astype(F32))
            for b in range(nb):
                lanes = slice(b * width, (b + 1) * width)
                out[:, lanes] = (q[rows, lanes].astype(F32) * scale[:, b : b + 1]).astype(BF16)

    return call(
        kernel,
        (jax.ShapeDtypeStruct((h, cols), BF16),) * 2,
        (quantized, exponents),
    )


def outer_update(average, momentum, outer_params):
    new_momentum = outer_decay * momentum + average
    new_params = outer_params - outer_rate * (average + outer_decay * new_momentum)
    return (new_momentum, new_params)


def outer_step(half, other, momentum, outer_params):
    n, cols = momentum.shape
    h = n // 2

    def kernel(a, b, m, p, new_m, new_p):
        j = pl.program_id(0)

        def update(total):
            average = total[...].astype(F32) / (N_X * N_ZL)
            new_m[...], new_p[...] = outer_update(average, m[...], p[...])

        pl.when(j == 0)(lambda: update(a))
        pl.when(j == 1)(lambda: update(b))

    def half_of(j):
        return (lax.rem(x_bit(1) + j, 2), 0)

    spec = pl.BlockSpec((h, cols), half_of)
    return call(
        kernel,
        (jax.ShapeDtypeStruct((n, cols), F32),) * 2,
        (half, other, momentum, outer_params),
        cost=2.0,
        grid=(2,),
        in_specs=[full((h, cols)), full((h, cols)), spec, spec],
        out_specs=(spec, spec),
    )


def after(values, *events):
    held = lax.optimization_barrier(tuple(values) + events)
    return held[: len(values)]


def shards(
    tokens, norm_gain, key_weight, key_cotangent, quantized, scale_exponent, momentum, outer_params
):
    gains = norm_gain
    cot = key_cotangent
    weight = key_weight[0]

    n_down = to_up(weight)
    n_up = to_down(weight)
    far_weight = to_far(weight)

    sent, extra_sent, ir = split_tokens(tokens, cot)
    other = to_core(sent)
    extra = to_core(extra_sent)

    n_down, n_up, quant, exponents = after((n_down, n_up, quantized[0], scale_exponent[0]), ir)
    keep, send = scaled_halves(quant, exponents)
    x1 = swap_x(send, 1)
    n_opposite = to_up(n_down)

    other, extra = after((other, extra), keep)
    hidden_far, f_opposite, f_minus, f_plus, f_own = partials(
        tokens, gains, cot, ir, other, extra, 1
    )
    f_step = to_down(f_opposite)
    f_from_down = to_up(f_plus)

    other, extra = after((other, extra), f_own)
    hidden_near, g_opposite, g_minus, g_plus, g_own = partials(
        tokens, gains, cot, ir, other, extra, 0
    )
    keep, x1 = after((keep, x1), g_own)
    half = keep + x1
    q = half.shape[0] // 2
    mine = x_bit(2) * q
    part = lax.dynamic_slice_in_dim(half, mine, q)
    x2 = swap_x(lax.dynamic_slice_in_dim(half, q - mine, q), 2)

    near_rows = (n_opposite, n_down, n_up, weight)
    *near_rows, hidden_near = after((*near_rows, hidden_near), part)
    near_keys = project(hidden_near, near_rows)

    f_minus, f_step, near_keys = after((f_minus, f_step), near_keys) + (near_keys,)
    f_minus = f_minus + f_step
    f_from_up = to_down(f_minus)
    part, x2 = after((part, x2), f_minus)
    part = part + x2
    z1 = swap_z(part, 1)

    (far_weight,) = after((far_weight,), part)
    a_down = to_up(far_weight)
    a_up = to_down(far_weight)
    part, z1 = after((part, z1), far_weight)
    part = part + z1
    z2 = swap_z(part, 2)

    f_own, f_from_down, f_from_up = after((f_own, f_from_down, f_from_up), part)
    f_total = side_sum(f_own, f_from_down, f_from_up)
    far_sum = to_far(f_total)
    (a_down,) = after((a_down,), f_total)
    a_opposite = to_up(a_down)
    part, z2 = after((part, z2), a_down)
    part = part + z2
    x3 = swap_x(part, 2)

    g_opposite, a_up = after((g_opposite, a_up), part)
    g_step = to_down(g_opposite)
    part, x3 = after((part, x3), a_up)
    pair = jnp.concatenate([part, x3])
    half = jnp.where(x_bit(2) == 0, pair, jnp.roll(pair, q, axis=0))
    x4 = swap_x(half, 1)
    g_plus, a_opposite = after((g_plus, a_opposite), half)
    g_from_down = to_up(g_plus)

    far_rows = (a_opposite, a_down, a_up, far_weight)
    keys_mine, keys_sent = project(hidden_far, far_rows, near_keys, cot, extra)
    arrived = to_core(keys_sent)
    g_minus, g_step = after((g_minus, g_step), keys_sent)
    g_minus = g_minus + g_step
    g_from_up = to_down(g_minus)
    half, x4 = after((half, x4), g_minus)
    new_momentum, new_params = outer_step(half, x4, momentum, outer_params)
    arrived, keys_mine = after((arrived, keys_mine), new_params)
    rows = tuple(near_rows) + tuple(far_rows)
    grad_sent, keys, mean = backward_other(other, extra, gains, keys_mine, arrived, rows)
    grad_arrived = to_core(grad_sent)
    (mean,) = after((mean,), grad_sent)
    token_grad = backward_own(tokens, gains, ir, cot, mean, rows)
    token_grad = fill_in(token_grad, grad_arrived)
    g_from_up, far_sum, token_grad = after((g_from_up, far_sum), token_grad) + (token_grad,)
    weight_grad, gain_grad = final_sum(g_own, g_from_down, g_from_up, far_sum, weight, gains)
    return (keys, token_grad, weight_grad[None], gain_grad, new_momentum, new_params)


def solution(mesh):
    return jax.shard_map(
        shards,
        mesh=mesh,
        in_specs=(
            P(("replica", "dp"), None),
            P("replica", None),
            P("replica", "dp", None),
            P(("replica", "dp"), None),
            P("replica", "dp", None),
            P("replica", "dp", None),
            P("dp", None),
            P("dp", None),
        ),
        out_specs=(
            P(("replica", "dp"), None),
            P(("replica", "dp"), None),
            P("replica", "dp", None),
            P("replica", "dp"),
            P("dp", None),
            P("dp", None),
        ),
        check_vma=False,
    )
```

```python
import jax
import jax.numpy as jnp
from jax import lax
from jax.experimental import pallas as pl
from jax.experimental.pallas import tpu as pltpu
from jax.sharding import PartitionSpec as P

epsilon = 1e-05
outer_decay = 0.9
outer_rate = 0.7

F32 = jnp.float32
BF16 = jnp.bfloat16
N_Y, N_ZH, N_CORE = 4, 2, 2
N_CHIP = N_Y * N_ZH
N_X, N_ZL = 4, 4
WEIGHT = 1e10
VMEM_LIMIT = 12 * 1024 * 1024


def dp_moves(dy=0, dz=0, dc=0):
    pairs = []
    for zh in range(N_ZH):
        for y in range(N_Y):
            for c in range(N_CORE):
                to = (((zh + dz) % N_ZH) * N_Y + (y + dy) % N_Y) * N_CORE + (c + dc) % N_CORE
                pairs.append(((zh * N_Y + y) * N_CORE + c, to))
    return pairs


def to_up(v):
    return lax.ppermute(v, "dp", dp_moves(dy=1))


def to_down(v):
    return lax.ppermute(v, "dp", dp_moves(dy=-1))


def to_far(v):
    return lax.ppermute(v, "dp", dp_moves(dz=1))


def to_core(v):
    return lax.ppermute(v, "dp", dp_moves(dc=1))


def swap_x(v, bit):
    return lax.ppermute(
        v, "replica", [(x * N_ZL + z, (x ^ bit) * N_ZL + z) for x in range(N_X) for z in range(N_ZL)]
    )


def swap_z(v, bit):
    return lax.ppermute(
        v, "replica", [(x * N_ZL + z, x * N_ZL + (z ^ bit)) for x in range(N_X) for z in range(N_ZL)]
    )


def core():
    return lax.rem(lax.axis_index("dp"), N_CORE)


def chip(side, dy):
    mine = lax.div(lax.axis_index("dp"), N_CORE)
    zh = lax.rem(lax.div(mine, N_Y) + side, N_ZH)
    return zh * N_Y + lax.rem(lax.rem(mine, N_Y) + dy, N_Y)


def place(side, dy):
    return chip(side, dy) * N_CORE + core()


def call(kernel, outs, ins, cost=1.0, vmem=VMEM_LIMIT, **kw):
    return pl.pallas_call(
        kernel,
        out_shape=outs,
        compiler_params=pltpu.CompilerParams(vmem_limit_bytes=vmem),
        cost_estimate=pl.CostEstimate(
            flops=int(cost * WEIGHT), bytes_accessed=0, transcendentals=0
        ),
        **kw,
    )(*ins)


HBM = pl.BlockSpec(memory_space=pltpu.HBM)
INSIDE = pl.BlockSpec(memory_space=pltpu.VMEM)


def full(shape):
    return pl.BlockSpec(shape, lambda j: (0,) * len(shape))


def block(index, size):
    return pl.ds(pl.multiple_of(index * size, size), size)


def dot_nt(a, b):
    return lax.dot_general(a, b, (((1,), (1,)), ((), ())), preferred_element_type=F32)


def dot(a, b):
    return jnp.dot(a, b, preferred_element_type=F32)


def identity(n):
    r = lax.broadcasted_iota(jnp.int32, (n, n), 0)
    c = lax.broadcasted_iota(jnp.int32, (n, n), 1)
    return jnp.where(r == c, 1.0, 0.0).astype(BF16)


def start_all(copies):
    for copy in copies:
        copy.start()
    return copies


ORDER = (2, 3, 1, 0)


def split_tokens(tokens, cot):
    t, d = tokens.shape
    f = cot.shape[1]
    steps = d // (2 * f)

    def kernel(tok, ct, mine, sent, extra, ir_out, sems):
        arrivals = []
        for i in range(steps):
            cols = slice(i * f, (i + 1) * f)
            arrivals += start_all(
                [
                    pltpu.make_async_copy(
                        tok.at[:, block(2 * i + core(), f)], mine.at[:, cols], sems.at[0, i]
                    ),
                    pltpu.make_async_copy(
                        tok.at[:, block(2 * i + 1 - core(), f)], sent.at[:, cols], sems.at[1, i]
                    ),
                ]
            )
        acc = jnp.zeros((t, 128), F32)
        for i in range(steps):
            arrivals[2 * i].wait()
            arrivals[2 * i + 1].wait()
            for n in range(i * f, (i + 1) * f, 128):
                for part in (mine, sent):
                    v = part[:, n : n + 128].astype(F32)
                    acc += v * v
        mean = jnp.sum(acc, axis=1, keepdims=True) / d
        ir = lax.rsqrt(jnp.broadcast_to(mean, (t, 128)) + epsilon)
        ir_out[...] = ir
        lane = lax.broadcasted_iota(jnp.int32, (t, 128), 1)
        terms = exact_terms(ir, lane, 0)
        extra[:, :f] = ct[...]
        extra[:, f:] = terms.astype(BF16)

    return call(
        kernel,
        (
            jax.ShapeDtypeStruct((t, d // 2), BF16),
            jax.ShapeDtypeStruct((t, d // 2), BF16),
            jax.ShapeDtypeStruct((t, f + 128), BF16),
            jax.ShapeDtypeStruct((t, 128), F32),
        ),
        (tokens, cot),
        cost=3.2,
        vmem=56 * 1024 * 1024,
        in_specs=[HBM, INSIDE],
        out_specs=(INSIDE,) * 4,
        scratch_shapes=[pltpu.SemaphoreType.DMA((2, steps))],
    )


def exact_terms(column, lane, first):
    high = column.astype(BF16).astype(F32)
    middle = (column - high).astype(BF16).astype(F32)
    low = column - high - middle
    zero = jnp.zeros_like(column)
    terms = jnp.where(lane == first, high, jnp.where(lane == first + 1, middle, zero))
    return jnp.where(lane == first + 2, low, terms)


def from_terms(values, first):
    return sum(values[:, first + i : first + i + 1].astype(F32) for i in range(3))


def partner_scale(extra, f):
    return from_terms(extra, f)


def hidden_block(hid, cols, own, oth, gain, irr, ext, side, dy):
    t = own.shape[0]
    f = cols.stop - cols.start
    g = gain[:, block(place(side, dy), f)]
    at = block(chip(side, dy), f)
    hid[:t, cols] = (own[:, at].astype(F32) * irr[:, 0:1] * g).astype(BF16)
    hid[t:, cols] = (oth[:, at].astype(F32) * partner_scale(ext, f) * g).astype(BF16)


def partials(mine, gains, cot, ir, other, extra, side):
    t = mine.shape[0]
    f = k = cot.shape[1]

    def kernel(own, oth, gain, ct, irr, ext, *refs):
        outs, hid, cot_t = refs[:4], refs[4], refs[5]
        eye = identity(k)
        cot_t[:, :t] = dot_nt(eye, ct[...]).astype(BF16)
        cot_t[:, t:] = dot_nt(eye, ext[:, :k]).astype(BF16)
        for i in range(N_Y):
            cols = slice(i * f, (i + 1) * f)
            hidden_block(hid, cols, own, oth, gain, irr, ext, side, ORDER[i])
            outs[i][...] = dot(cot_t[...], hid[:, cols]).astype(BF16)

    shape = jax.ShapeDtypeStruct((k, f), BF16)
    hidden = [] if side else [jax.ShapeDtypeStruct((2 * t, N_Y * f), BF16)]
    scratch = [pltpu.VMEM((2 * t, N_Y * f), BF16)] if side else []
    return call(
        kernel,
        [shape] * 4 + hidden,
        (mine, other, gains, cot, ir, extra),
        cost=3.4,
        in_specs=[INSIDE] * 6,
        out_specs=[INSIDE] * (4 + len(hidden)),
        scratch_shapes=scratch + [pltpu.VMEM((k, 2 * t), BF16)],
    )


def side_sum(own, from_down, from_up):
    def kernel(o, a, b, out):
        out[...] = (o[...].astype(F32) + a[...].astype(F32) + b[...].astype(F32)).astype(BF16)

    return call(kernel, jax.ShapeDtypeStruct(own.shape, BF16), (own, from_down, from_up), cost=1.0)


def final_sum(own, from_down, from_up, far, weight, gains):
    k, f = own.shape

    def kernel(o, a, b, fr, w, gain, out, gain_out):
        eye = identity(k)
        weight_t = dot_nt(eye, w[...])
        total = (o[...].astype(F32) + a[...].astype(F32)) + (b[...].astype(F32) + fr[...].astype(F32))
        out[...] = dot_nt(eye, total.astype(BF16)).astype(BF16)
        sums = jnp.sum(total * weight_t, axis=0, keepdims=True)
        gain_out[...] = (sums / gain[:, block(lax.axis_index("dp"), f)]).astype(BF16)

    return call(
        kernel,
        (jax.ShapeDtypeStruct((f, k), BF16), jax.ShapeDtypeStruct((1, f), BF16)),
        (own, from_down, from_up, far, weight, gains),
        cost=2.9,
    )


def project_near(hidden, weights):
    f, k = weights[0].shape

    def kernel(hid, w0, w1, w2, w3, out):
        total = jnp.zeros(out.shape, F32)
        for i, w in enumerate((w0, w1, w2, w3)):
            total += dot(hid[:, i * f : (i + 1) * f], w[...])
        out[...] = total

    return call(
        kernel,
        jax.ShapeDtypeStruct((hidden.shape[0], k), F32),
        (hidden,) + tuple(weights),
        cost=2.5,
        in_specs=[INSIDE] * 5,
        out_specs=INSIDE,
    )


def project_far(mine, other, gains, ir, extra, cot, weights, before):
    f, k = weights[0].shape
    t = mine.shape[0]

    def kernel(own_x, oth, gain, irr, ext, ct, w0, w1, w2, w3, first, kept, sent, hid):
        total = first[...]
        for i, w in enumerate((w0, w1, w2, w3)):
            cols = slice(i * f, (i + 1) * f)
            hidden_block(hid, cols, own_x, oth, gain, irr, ext, 1, ORDER[i])
            total += dot(hid[:, cols], w[...])
        own = jnp.sum(total[:t] * ct[...].astype(F32), axis=1, keepdims=True)
        others = jnp.sum(total[t:] * ext[:, :k].astype(F32), axis=1, keepdims=True)
        lane = lax.broadcasted_iota(jnp.int32, (t, 128), 1)
        kept[:, :k] = total[:t]
        kept[:, k:] = jnp.where(lane == 0, own, others)
        sent[:, :k] = total[t:].astype(BF16)
        sent[:, k:] = (exact_terms(others, lane, 0) + exact_terms(own, lane, 3)).astype(BF16)

    return call(
        kernel,
        (
            jax.ShapeDtypeStruct((t, k + 128), F32),
            jax.ShapeDtypeStruct((t, k + 128), BF16),
        ),
        (mine, other, gains, ir, extra, cot) + tuple(weights) + (before,),
        cost=2.5,
        in_specs=[INSIDE] * 11,
        out_specs=(INSIDE,) * 2,
        scratch_shapes=[pltpu.VMEM((2 * t, N_Y * f), BF16)],
    )


def blocks_of_chip():
    return [(side, dy) for side in range(N_ZH) for dy in ORDER]


def token_gradient(x, ws, gain, ct, scale, mean, store):
    f = ws[0].shape[0]
    shift = scale * scale * mean
    for i, (side, dy) in enumerate(blocks_of_chip()):
        g = gain[:, block(place(side, dy), f)]
        grad = dot_nt(ct, ws[i][...])
        values = x[:, block(chip(side, dy), f)].astype(F32)
        store(i, (scale * (grad * g) - values * shift).astype(BF16))


def backward_other(other, extra, gains, mine, arrived, weights):
    t = other.shape[0]
    f = k = extra.shape[1] - 128
    d = gains.shape[1]

    def kernel(*refs):
        oth, gain, ext, mn, arr = refs[:5]
        ws = refs[5:13]
        out, keys, mean = refs[13:16]
        keys[...] = (mn[:, :k] + arr[:, :k].astype(F32)).astype(BF16)
        own = (mn[:, k : k + 1] + from_terms(arr, k)) / d
        others = (mn[:, k + 1 : k + 2] + from_terms(arr, k + 3)) / d
        mean[...] = jnp.broadcast_to(own, (t, 128))

        def store(i, values):
            out[:, i * f : (i + 1) * f] = values

        token_gradient(oth, ws, gain, ext[:, :k], partner_scale(ext, f), others, store)

    return call(
        kernel,
        (
            jax.ShapeDtypeStruct((t, d // 2), BF16),
            jax.ShapeDtypeStruct((t, k), BF16),
            jax.ShapeDtypeStruct((t, 128), F32),
        ),
        (other, gains, extra, mine, arrived) + tuple(weights),
        cost=5.5,
        in_specs=[INSIDE] * 13,
        out_specs=(INSIDE,) * 3,
    )


def backward_own(mine, gains, ir, cot, mean, weights):
    t = mine.shape[0]
    d = gains.shape[1]
    f = cot.shape[1]
    where = blocks_of_chip()

    def kernel(*refs):
        own, gain, irr, ct, mn = refs[:5]
        ws = refs[5:13]
        out, results, sems = refs[13:]
        leaving = []

        def store(i, values):
            results[i] = values
            to = out.at[:, block(place(*where[i]), f)]
            leaving.extend(start_all([pltpu.make_async_copy(results.at[i], to, sems.at[i])]))

        token_gradient(own, ws, gain, ct[...], irr[:, 0:1], mn[:, 0:1], store)
        for copy in leaving:
            copy.wait()

    return call(
        kernel,
        jax.ShapeDtypeStruct((t, d), BF16),
        (mine, gains, ir, cot, mean) + tuple(weights),
        cost=4.7,
        in_specs=[INSIDE] * 13,
        out_specs=HBM,
        scratch_shapes=[
            pltpu.VMEM((N_CHIP, t, f), BF16),
            pltpu.SemaphoreType.DMA((N_CHIP,)),
        ],
    )


def fill_in(token_grad, arrived):
    f = arrived.shape[1] // N_CHIP
    where = blocks_of_chip()

    def kernel(_, arr, out, sems):
        away = 1 - core()
        leaving = []
        for i in range(N_CHIP):
            to = out.at[:, block(chip(*where[i]) * N_CORE + away, f)]
            leaving += start_all(
                [pltpu.make_async_copy(arr.at[:, i * f : (i + 1) * f], to, sems.at[i])]
            )
        for copy in leaving:
            copy.wait()

    return call(
        kernel,
        jax.ShapeDtypeStruct(token_grad.shape, token_grad.dtype),
        (token_grad, arrived),
        cost=1.4,
        in_specs=[HBM, INSIDE],
        out_specs=HBM,
        input_output_aliases={0: 0},
        scratch_shapes=[pltpu.SemaphoreType.DMA((N_CHIP,))],
    )


def x_bit(bit):
    return lax.rem(lax.div(lax.axis_index("replica"), N_ZL * bit), 2)


def scaled_halves(quantized, exponents):
    n, cols = quantized.shape
    h = n // 2
    nb = exponents.shape[0]
    width = cols // nb

    def kernel(q, e, keep, send, scales):
        powers = jnp.exp2(e[...].astype(F32)).astype(BF16)
        scales[...] = dot_nt(identity(n), powers)
        for out, half in ((keep, x_bit(1)), (send, 1 - x_bit(1))):
            rows = block(half, h)
            for b in range(nb):
                lanes = slice(b * width, (b + 1) * width)
                scale = scales[rows, b : b + 1]
                out[:, lanes] = (q[rows, lanes].astype(F32) * scale).astype(BF16)

    return call(
        kernel,
        (jax.ShapeDtypeStruct((h, cols), BF16),) * 2,
        (quantized, exponents),
        cost=20.0,
        scratch_shapes=[pltpu.VMEM((n, nb), F32)],
    )


def outer_update(average, momentum, outer_params):
    new_momentum = outer_decay * momentum + average
    new_params = outer_params - outer_rate * (average + outer_decay * new_momentum)
    return (new_momentum, new_params)


def outer_step(half, other, momentum, outer_params):
    n, cols = momentum.shape
    h = n // 2

    def kernel(a, b, m, p, new_m, new_p):
        j = pl.program_id(0)

        def update(total):
            average = total[...].astype(F32) / (N_X * N_ZL)
            new_m[...], new_p[...] = outer_update(average, m[...], p[...])

        pl.when(j == 0)(lambda: update(a))
        pl.when(j == 1)(lambda: update(b))

    def half_of(j):
        return (lax.rem(x_bit(1) + j, 2), 0)

    spec = pl.BlockSpec((h, cols), half_of)
    return call(
        kernel,
        (jax.ShapeDtypeStruct((n, cols), F32),) * 2,
        (half, other, momentum, outer_params),
        cost=2.0,
        grid=(2,),
        in_specs=[full((h, cols)), full((h, cols)), spec, spec],
        out_specs=(spec, spec),
    )


def after(values, *events):
    held = lax.optimization_barrier(tuple(values) + events)
    return held[: len(values)]


def shards(
    tokens, norm_gain, key_weight, key_cotangent, quantized, scale_exponent, momentum, outer_params
):
    gains = norm_gain
    cot = key_cotangent
    weight = key_weight[0]

    n_down = to_up(weight)
    n_up = to_down(weight)

    mine, sent, extra_sent, ir = split_tokens(tokens, cot)
    other = to_core(sent)
    extra = to_core(extra_sent)

    quant, exponents = after((quantized[0], scale_exponent[0]), ir)
    keep, send = scaled_halves(quant, exponents.T)
    x1 = swap_x(send, 1)
    far_weight = to_far(after((weight,), keep)[0])

    other, extra = after((other, extra), keep)
    f_opposite, f_minus, f_plus, f_own = partials(
        mine, gains, cot, ir, other, extra, 1
    )
    n_down, n_up = after((n_down, n_up), f_own)
    n_opposite = to_up(n_down)
    f_step = to_down(f_opposite)
    f_from_down = to_up(f_plus)

    keep, x1 = after((keep, x1), n_up)
    half = keep + x1
    q = half.shape[0] // 2
    first = x_bit(2) * q
    part = lax.dynamic_slice_in_dim(half, first, q)
    x2 = swap_x(lax.dynamic_slice_in_dim(half, q - first, q), 2)

    other, extra = after((other, extra), part)
    g_opposite, g_minus, g_plus, g_own, hidden_near = partials(
        mine, gains, cot, ir, other, extra, 0
    )
    part, x2 = after((part, x2), g_own)
    part = part + x2
    z1 = swap_z(part, 1)

    f_minus, f_step = after((f_minus, f_step), part)
    f_minus = f_minus + f_step
    f_from_up = to_down(f_minus)

    near_rows = (n_opposite, n_down, n_up, weight)
    *near_rows, hidden_near = after((*near_rows, hidden_near), f_minus)
    near_keys = project_near(hidden_near, near_rows)
    part, z1 = after((part, z1), near_keys)
    part = part + z1
    z2 = swap_z(part, 2)

    (far_weight,) = after((far_weight,), part)
    a_down = to_up(far_weight)
    a_up = to_down(far_weight)

    f_own, f_from_down, f_from_up = after((f_own, f_from_down, f_from_up), far_weight)
    f_total = side_sum(f_own, f_from_down, f_from_up)
    far_sum = to_far(f_total)
    part, z2 = after((part, z2), f_total)
    part = part + z2
    x3 = swap_x(part, 2)
    (a_down,) = after((a_down,), part)
    a_opposite = to_up(a_down)

    g_opposite, a_up = after((g_opposite, a_up), a_down)
    g_step = to_down(g_opposite)
    part, x3 = after((part, x3), a_up)
    pair = jnp.concatenate([part, x3])
    half = jnp.where(x_bit(2) == 0, pair, jnp.roll(pair, q, axis=0))
    x4 = swap_x(half, 1)
    g_plus, a_opposite = after((g_plus, a_opposite), half)
    g_from_down = to_up(g_plus)

    far_rows = (a_opposite, a_down, a_up, far_weight)
    keys_mine, keys_sent = project_far(
        mine, other, gains, ir, extra, cot, far_rows, near_keys
    )
    arrived = to_core(keys_sent)
    half, x4 = after((half, x4), keys_sent)
    new_momentum, new_params = outer_step(half, x4, momentum, outer_params)
    g_minus, g_step = after((g_minus, g_step), new_params)
    g_minus = g_minus + g_step
    g_from_up = to_down(g_minus)
    arrived, keys_mine, far_sum = after((arrived, keys_mine, far_sum), g_minus)
    rows = tuple(near_rows) + tuple(far_rows)
    grad_sent, keys, mean = backward_other(other, extra, gains, keys_mine, arrived, rows)
    grad_arrived = to_core(grad_sent)
    mean, far_sum = after((mean, far_sum), grad_sent)
    token_grad = backward_own(mine, gains, ir, cot, mean, rows)
    grad_arrived, token_grad = after((grad_arrived, token_grad), new_params)
    token_grad = fill_in(token_grad, grad_arrived)
    (g_from_up,) = after((g_from_up,), token_grad)
    weight_grad, gain_grad = final_sum(g_own, g_from_down, g_from_up, far_sum, weight, gains)
    return (keys, token_grad, weight_grad[None], gain_grad, new_momentum, new_params)


def solution(mesh):
    return jax.shard_map(
        shards,
        mesh=mesh,
        in_specs=(
            P(("replica", "dp"), None),
            P("replica", None),
            P("replica", "dp", None),
            P(("replica", "dp"), None),
            P("replica", "dp", None),
            P("replica", "dp", None),
            P("dp", None),
            P("dp", None),
        ),
        out_specs=(
            P(("replica", "dp"), None),
            P(("replica", "dp"), None),
            P("replica", "dp", None),
            P("replica", "dp"),
            P("dp", None),
            P("dp", None),
        ),
        check_vma=False,
    )
```

```python
import jax
import jax.numpy as jnp
from jax import lax
from jax.experimental import pallas as pl
from jax.experimental.pallas import tpu as pltpu
from jax.sharding import PartitionSpec as P

epsilon = 1e-05
outer_decay = 0.9
outer_rate = 0.7

F32 = jnp.float32
BF16 = jnp.bfloat16
N_Y, N_ZH, N_CORE = 4, 2, 2
N_CHIP = N_Y * N_ZH
N_X, N_ZL = 4, 4
WEIGHT = 1e10
VMEM_LIMIT = 12 * 1024 * 1024


def dp_moves(dy=0, dz=0, dc=0):
    pairs = []
    for zh in range(N_ZH):
        for y in range(N_Y):
            for c in range(N_CORE):
                to = (((zh + dz) % N_ZH) * N_Y + (y + dy) % N_Y) * N_CORE + (c + dc) % N_CORE
                pairs.append(((zh * N_Y + y) * N_CORE + c, to))
    return pairs


def to_up(v):
    return lax.ppermute(v, "dp", dp_moves(dy=1))


def to_down(v):
    return lax.ppermute(v, "dp", dp_moves(dy=-1))


def to_far(v):
    return lax.ppermute(v, "dp", dp_moves(dz=1))


def to_core(v):
    return lax.ppermute(v, "dp", dp_moves(dc=1))


def swap_x(v, bit):
    return lax.ppermute(
        v, "replica", [(x * N_ZL + z, (x ^ bit) * N_ZL + z) for x in range(N_X) for z in range(N_ZL)]
    )


def swap_z(v, bit):
    return lax.ppermute(
        v, "replica", [(x * N_ZL + z, x * N_ZL + (z ^ bit)) for x in range(N_X) for z in range(N_ZL)]
    )


def core():
    return lax.rem(lax.axis_index("dp"), N_CORE)


def chip(side, dy):
    mine = lax.div(lax.axis_index("dp"), N_CORE)
    zh = lax.rem(lax.div(mine, N_Y) + side, N_ZH)
    return zh * N_Y + lax.rem(lax.rem(mine, N_Y) + dy, N_Y)


def place(side, dy):
    return chip(side, dy) * N_CORE + core()


def call(kernel, outs, ins, cost=1.0, vmem=VMEM_LIMIT, **kw):
    return pl.pallas_call(
        kernel,
        out_shape=outs,
        compiler_params=pltpu.CompilerParams(vmem_limit_bytes=vmem),
        cost_estimate=pl.CostEstimate(
            flops=int(cost * WEIGHT), bytes_accessed=0, transcendentals=0
        ),
        **kw,
    )(*ins)


HBM = pl.BlockSpec(memory_space=pltpu.HBM)
INSIDE = pl.BlockSpec(memory_space=pltpu.VMEM)


def full(shape):
    return pl.BlockSpec(shape, lambda j: (0,) * len(shape))


def block(index, size):
    return pl.ds(pl.multiple_of(index * size, size), size)


def dot_nt(a, b):
    return lax.dot_general(a, b, (((1,), (1,)), ((), ())), preferred_element_type=F32)


def dot(a, b):
    return jnp.dot(a, b, preferred_element_type=F32)


def identity(n):
    r = lax.broadcasted_iota(jnp.int32, (n, n), 0)
    c = lax.broadcasted_iota(jnp.int32, (n, n), 1)
    return jnp.where(r == c, 1.0, 0.0).astype(BF16)


def start_all(copies):
    for copy in copies:
        copy.start()
    return copies


ORDER = (2, 3, 1, 0)


def split_tokens(tokens, cot):
    t, d = tokens.shape
    f = cot.shape[1]
    steps = d // (2 * f)

    def kernel(tok, ct, mine, sent, extra, ir_out, sems):
        arrivals = []
        for i in range(steps):
            cols = slice(i * f, (i + 1) * f)
            arrivals += start_all(
                [
                    pltpu.make_async_copy(
                        tok.at[:, block(2 * i + core(), f)], mine.at[:, cols], sems.at[0, i]
                    ),
                    pltpu.make_async_copy(
                        tok.at[:, block(2 * i + 1 - core(), f)], sent.at[:, cols], sems.at[1, i]
                    ),
                ]
            )
        acc = jnp.zeros((t, 128), F32)
        for i in range(steps):
            arrivals[2 * i].wait()
            arrivals[2 * i + 1].wait()
            for n in range(i * f, (i + 1) * f, 128):
                for part in (mine, sent):
                    v = part[:, n : n + 128].astype(F32)
                    acc += v * v
        mean = jnp.sum(acc, axis=1, keepdims=True) / d
        ir = lax.rsqrt(jnp.broadcast_to(mean, (t, 128)) + epsilon)
        ir_out[...] = ir
        lane = lax.broadcasted_iota(jnp.int32, (t, 128), 1)
        terms = exact_terms(ir, lane, 0)
        extra[:, :f] = ct[...]
        extra[:, f:] = terms.astype(BF16)

    return call(
        kernel,
        (
            jax.ShapeDtypeStruct((t, d // 2), BF16),
            jax.ShapeDtypeStruct((t, d // 2), BF16),
            jax.ShapeDtypeStruct((t, f + 128), BF16),
            jax.ShapeDtypeStruct((t, 128), F32),
        ),
        (tokens, cot),
        cost=3.2,
        vmem=56 * 1024 * 1024,
        in_specs=[HBM, INSIDE],
        out_specs=(INSIDE,) * 4,
        scratch_shapes=[pltpu.SemaphoreType.DMA((2, steps))],
    )


def exact_terms(column, lane, first):
    high = column.astype(BF16).astype(F32)
    middle = (column - high).astype(BF16).astype(F32)
    low = column - high - middle
    zero = jnp.zeros_like(column)
    terms = jnp.where(lane == first, high, jnp.where(lane == first + 1, middle, zero))
    return jnp.where(lane == first + 2, low, terms)


def from_terms(values, first):
    return sum(values[:, first + i : first + i + 1].astype(F32) for i in range(3))


def partner_scale(extra, f):
    return from_terms(extra, f)


def hidden_block(hid, cols, own, oth, gain, irr, ext, side, dy):
    t = own.shape[0]
    f = cols.stop - cols.start
    g = gain[:, block(place(side, dy), f)]
    at = block(chip(side, dy), f)
    hid[:t, cols] = (own[:, at].astype(F32) * irr[:, 0:1] * g).astype(BF16)
    hid[t:, cols] = (oth[:, at].astype(F32) * partner_scale(ext, f) * g).astype(BF16)


def partials(mine, gains, cot, ir, other, extra, side):
    t = mine.shape[0]
    f = k = cot.shape[1]

    def kernel(own, oth, gain, ct, irr, ext, *refs):
        outs, hid, cot_t = refs[:4], refs[4], refs[5]
        eye = identity(k)
        cot_t[:, :t] = dot_nt(eye, ct[...]).astype(BF16)
        cot_t[:, t:] = dot_nt(eye, ext[:, :k]).astype(BF16)
        for i in range(N_Y):
            cols = slice(i * f, (i + 1) * f)
            hidden_block(hid, cols, own, oth, gain, irr, ext, side, ORDER[i])
            outs[i][...] = dot(cot_t[...], hid[:, cols]).astype(BF16)

    shape = jax.ShapeDtypeStruct((k, f), BF16)
    hidden = [] if side else [jax.ShapeDtypeStruct((2 * t, N_Y * f), BF16)]
    scratch = [pltpu.VMEM((2 * t, N_Y * f), BF16)] if side else []
    return call(
        kernel,
        [shape] * 4 + hidden,
        (mine, other, gains, cot, ir, extra),
        cost=3.4,
        in_specs=[INSIDE] * 6,
        out_specs=[INSIDE] * (4 + len(hidden)),
        scratch_shapes=scratch + [pltpu.VMEM((k, 2 * t), BF16)],
    )


def side_sum(own, from_down, from_up):
    def kernel(o, a, b, out):
        out[...] = (o[...].astype(F32) + a[...].astype(F32) + b[...].astype(F32)).astype(BF16)

    return call(kernel, jax.ShapeDtypeStruct(own.shape, BF16), (own, from_down, from_up), cost=1.0)


def final_sum(own, from_down, from_up, far, weight, gains):
    k, f = own.shape

    def kernel(o, a, b, fr, w, gain, out, gain_out):
        eye = identity(k)
        weight_t = dot_nt(eye, w[...])
        total = (o[...].astype(F32) + a[...].astype(F32)) + (b[...].astype(F32) + fr[...].astype(F32))
        out[...] = dot_nt(eye, total.astype(BF16)).astype(BF16)
        sums = jnp.sum(total * weight_t, axis=0, keepdims=True)
        gain_out[...] = (sums / gain[:, block(lax.axis_index("dp"), f)]).astype(BF16)

    return call(
        kernel,
        (jax.ShapeDtypeStruct((f, k), BF16), jax.ShapeDtypeStruct((1, f), BF16)),
        (own, from_down, from_up, far, weight, gains),
        cost=2.9,
    )


def project_near(hidden, weights):
    f, k = weights[0].shape

    def kernel(hid, w0, w1, w2, w3, out):
        total = jnp.zeros(out.shape, F32)
        for i, w in enumerate((w0, w1, w2, w3)):
            total += dot(hid[:, i * f : (i + 1) * f], w[...])
        out[...] = total

    return call(
        kernel,
        jax.ShapeDtypeStruct((hidden.shape[0], k), F32),
        (hidden,) + tuple(weights),
        cost=2.5,
        in_specs=[INSIDE] * 5,
        out_specs=INSIDE,
    )


def project_far(mine, other, gains, ir, extra, cot, weights, before):
    f, k = weights[0].shape
    t = mine.shape[0]

    def kernel(own_x, oth, gain, irr, ext, ct, w0, w1, w2, w3, first, kept, sent, hid):
        total = first[...]
        for i, w in enumerate((w0, w1, w2, w3)):
            cols = slice(i * f, (i + 1) * f)
            hidden_block(hid, cols, own_x, oth, gain, irr, ext, 1, ORDER[i])
            total += dot(hid[:, cols], w[...])
        own = jnp.sum(total[:t] * ct[...].astype(F32), axis=1, keepdims=True)
        others = jnp.sum(total[t:] * ext[:, :k].astype(F32), axis=1, keepdims=True)
        lane = lax.broadcasted_iota(jnp.int32, (t, 128), 1)
        kept[:, :k] = total[:t]
        kept[:, k:] = jnp.where(lane == 0, own, others)
        sent[:, :k] = total[t:].astype(BF16)
        sent[:, k:] = (exact_terms(others, lane, 0) + exact_terms(own, lane, 3)).astype(BF16)

    return call(
        kernel,
        (
            jax.ShapeDtypeStruct((t, k + 128), F32),
            jax.ShapeDtypeStruct((t, k + 128), BF16),
        ),
        (mine, other, gains, ir, extra, cot) + tuple(weights) + (before,),
        cost=2.5,
        in_specs=[INSIDE] * 11,
        out_specs=(INSIDE,) * 2,
        scratch_shapes=[pltpu.VMEM((2 * t, N_Y * f), BF16)],
    )


def blocks_of_chip():
    return [(side, dy) for side in range(N_ZH) for dy in ORDER]


def token_gradient(x, ws, gain, ct, scale, mean, store):
    f = ws[0].shape[0]
    shift = scale * scale * mean
    for i, (side, dy) in enumerate(blocks_of_chip()):
        g = gain[:, block(place(side, dy), f)]
        grad = dot_nt(ct, ws[i][...])
        values = x[:, block(chip(side, dy), f)].astype(F32)
        store(i, (scale * (grad * g) - values * shift).astype(BF16))


def backward_other(other, extra, gains, mine, arrived, weights):
    t = other.shape[0]
    f = k = extra.shape[1] - 128
    d = gains.shape[1]

    def kernel(*refs):
        oth, gain, ext, mn, arr = refs[:5]
        ws = refs[5:13]
        out, keys, mean = refs[13:16]
        keys[...] = (mn[:, :k] + arr[:, :k].astype(F32)).astype(BF16)
        own = (mn[:, k : k + 1] + from_terms(arr, k)) / d
        others = (mn[:, k + 1 : k + 2] + from_terms(arr, k + 3)) / d
        mean[...] = jnp.broadcast_to(own, (t, 128))

        def store(i, values):
            out[:, i * f : (i + 1) * f] = values

        token_gradient(oth, ws, gain, ext[:, :k], partner_scale(ext, f), others, store)

    return call(
        kernel,
        (
            jax.ShapeDtypeStruct((t, d // 2), BF16),
            jax.ShapeDtypeStruct((t, k), BF16),
            jax.ShapeDtypeStruct((t, 128), F32),
        ),
        (other, gains, extra, mine, arrived) + tuple(weights),
        cost=5.5,
        in_specs=[INSIDE] * 13,
        out_specs=(INSIDE,) * 3,
    )


def backward_own(mine, gains, ir, cot, mean, weights):
    t = mine.shape[0]
    d = gains.shape[1]
    f = cot.shape[1]
    where = blocks_of_chip()

    def kernel(*refs):
        own, gain, irr, ct, mn = refs[:5]
        ws = refs[5:13]
        out, results, sems = refs[13:]
        leaving = []

        def store(i, values):
            results[i] = values
            to = out.at[:, block(place(*where[i]), f)]
            leaving.extend(start_all([pltpu.make_async_copy(results.at[i], to, sems.at[i])]))

        token_gradient(own, ws, gain, ct[...], irr[:, 0:1], mn[:, 0:1], store)
        for copy in leaving:
            copy.wait()

    return call(
        kernel,
        jax.ShapeDtypeStruct((t, d), BF16),
        (mine, gains, ir, cot, mean) + tuple(weights),
        cost=4.7,
        in_specs=[INSIDE] * 13,
        out_specs=HBM,
        scratch_shapes=[
            pltpu.VMEM((N_CHIP, t, f), BF16),
            pltpu.SemaphoreType.DMA((N_CHIP,)),
        ],
    )


def fill_in(token_grad, arrived):
    f = arrived.shape[1] // N_CHIP
    where = blocks_of_chip()

    def kernel(_, arr, out, sems):
        away = 1 - core()
        leaving = []
        for i in range(N_CHIP):
            to = out.at[:, block(chip(*where[i]) * N_CORE + away, f)]
            leaving += start_all(
                [pltpu.make_async_copy(arr.at[:, i * f : (i + 1) * f], to, sems.at[i])]
            )
        for copy in leaving:
            copy.wait()

    return call(
        kernel,
        jax.ShapeDtypeStruct(token_grad.shape, token_grad.dtype),
        (token_grad, arrived),
        cost=1.4,
        in_specs=[HBM, INSIDE],
        out_specs=HBM,
        input_output_aliases={0: 0},
        scratch_shapes=[pltpu.SemaphoreType.DMA((N_CHIP,))],
    )


def x_bit(bit):
    return lax.rem(lax.div(lax.axis_index("replica"), N_ZL * bit), 2)


def scaled_halves(quantized, exponents):
    n, cols = quantized.shape
    h = n // 2
    nb = exponents.shape[0]
    width = cols // nb

    def kernel(q, e, keep, send, scales):
        powers = jnp.exp2(e[...].astype(F32)).astype(BF16)
        scales[...] = dot_nt(identity(n), powers)
        for out, half in ((keep, x_bit(1)), (send, 1 - x_bit(1))):
            rows = block(half, h)
            for b in range(nb):
                lanes = slice(b * width, (b + 1) * width)
                scale = scales[rows, b : b + 1]
                out[:, lanes] = (q[rows, lanes].astype(F32) * scale).astype(BF16)

    return call(
        kernel,
        (jax.ShapeDtypeStruct((h, cols), BF16),) * 2,
        (quantized, exponents),
        cost=1.0,
        scratch_shapes=[pltpu.VMEM((n, nb), F32)],
    )


def outer_update(average, momentum, outer_params):
    new_momentum = outer_decay * momentum + average
    new_params = outer_params - outer_rate * (average + outer_decay * new_momentum)
    return (new_momentum, new_params)


def outer_step(half, other, momentum, outer_params):
    n, cols = momentum.shape
    h = n // 2

    def kernel(a, b, m, p, new_m, new_p):
        j = pl.program_id(0)

        def update(total):
            average = total[...].astype(F32) / (N_X * N_ZL)
            new_m[...], new_p[...] = outer_update(average, m[...], p[...])

        pl.when(j == 0)(lambda: update(a))
        pl.when(j == 1)(lambda: update(b))

    def half_of(j):
        return (lax.rem(x_bit(1) + j, 2), 0)

    spec = pl.BlockSpec((h, cols), half_of)
    return call(
        kernel,
        (jax.ShapeDtypeStruct((n, cols), F32),) * 2,
        (half, other, momentum, outer_params),
        cost=2.0,
        grid=(2,),
        in_specs=[full((h, cols)), full((h, cols)), spec, spec],
        out_specs=(spec, spec),
    )


def after(values, *events):
    held = lax.optimization_barrier(tuple(values) + events)
    return held[: len(values)]


def shards(
    tokens, norm_gain, key_weight, key_cotangent, quantized, scale_exponent, momentum, outer_params
):
    gains = norm_gain
    cot = key_cotangent
    weight = key_weight[0]

    n_down = to_up(weight)
    n_up = to_down(weight)

    mine, sent, extra_sent, ir = split_tokens(tokens, cot)
    other = to_core(sent)
    extra = to_core(extra_sent)

    quant, exponents = after((quantized[0], scale_exponent[0]), ir)
    keep, send = scaled_halves(quant, exponents.T)
    x1 = swap_x(send, 1)
    far_weight = to_far(after((weight,), keep)[0])

    other, extra = after((other, extra), keep)
    f_opposite, f_minus, f_plus, f_own = partials(
        mine, gains, cot, ir, other, extra, 1
    )
    n_down, n_up = after((n_down, n_up), f_own)
    n_opposite = to_up(n_down)
    f_step = to_down(f_opposite)
    f_from_down = to_up(f_plus)

    keep, x1 = after((keep, x1), n_up)
    part = keep + x1
    x2 = swap_x(part, 2)

    other, extra = after((other, extra), part)
    g_opposite, g_minus, g_plus, g_own, hidden_near = partials(
        mine, gains, cot, ir, other, extra, 0
    )
    part, x2 = after((part, x2), g_own)
    part = part + x2
    z1 = swap_z(part, 1)

    f_minus, f_step = after((f_minus, f_step), part)
    f_minus = f_minus + f_step
    f_from_up = to_down(f_minus)

    near_rows = (n_opposite, n_down, n_up, weight)
    *near_rows, hidden_near = after((*near_rows, hidden_near), f_minus)
    near_keys = project_near(hidden_near, near_rows)

    (far_weight,) = after((far_weight,), near_keys)
    a_down = to_up(far_weight)
    a_up = to_down(far_weight)
    part, z1 = after((part, z1), far_weight)
    part = part + z1
    z2 = swap_z(part, 2)

    f_own, f_from_down, f_from_up = after((f_own, f_from_down, f_from_up), part)
    f_total = side_sum(f_own, f_from_down, f_from_up)
    far_sum = to_far(f_total)
    part, z2 = after((part, z2), f_total)
    part = part + z2
    x3 = swap_x(part, 1)
    (a_down,) = after((a_down,), part)
    a_opposite = to_up(a_down)

    g_opposite, a_up = after((g_opposite, a_up), a_down)
    g_step = to_down(g_opposite)
    g_plus, a_opposite = after((g_plus, a_opposite), a_up)
    g_from_down = to_up(g_plus)

    far_rows = (a_opposite, a_down, a_up, far_weight)
    keys_mine, keys_sent = project_far(
        mine, other, gains, ir, extra, cot, far_rows, near_keys
    )
    arrived = to_core(keys_sent)
    part, x3 = after((part, x3), keys_sent)
    new_momentum, new_params = outer_step(part, x3, momentum, outer_params)
    g_minus, g_step = after((g_minus, g_step), new_params)
    g_minus = g_minus + g_step
    g_from_up = to_down(g_minus)
    arrived, keys_mine, far_sum = after((arrived, keys_mine, far_sum), g_minus)
    rows = tuple(near_rows) + tuple(far_rows)
    grad_sent, keys, mean = backward_other(other, extra, gains, keys_mine, arrived, rows)
    grad_arrived = to_core(grad_sent)
    mean, far_sum = after((mean, far_sum), grad_sent)
    token_grad = backward_own(mine, gains, ir, cot, mean, rows)
    grad_arrived, token_grad = after((grad_arrived, token_grad), new_params)
    token_grad = fill_in(token_grad, grad_arrived)
    (g_from_up,) = after((g_from_up,), token_grad)
    weight_grad, gain_grad = final_sum(g_own, g_from_down, g_from_up, far_sum, weight, gains)
    return (keys, token_grad, weight_grad[None], gain_grad, new_momentum, new_params)


def solution(mesh):
    return jax.shard_map(
        shards,
        mesh=mesh,
        in_specs=(
            P(("replica", "dp"), None),
            P("replica", None),
            P("replica", "dp", None),
            P(("replica", "dp"), None),
            P("replica", "dp", None),
            P("replica", "dp", None),
            P("dp", None),
            P("dp", None),
        ),
        out_specs=(
            P(("replica", "dp"), None),
            P(("replica", "dp"), None),
            P("replica", "dp", None),
            P("replica", "dp"),
            P("dp", None),
            P("dp", None),
        ),
        check_vma=False,
    )
```

```python
import jax
import jax.numpy as jnp
from jax import lax
from jax.experimental import pallas as pl
from jax.experimental.pallas import tpu as pltpu
from jax.sharding import PartitionSpec as P

epsilon = 1e-05
outer_decay = 0.9
outer_rate = 0.7

F32 = jnp.float32
BF16 = jnp.bfloat16
N_Y, N_ZH, N_CORE = 4, 2, 2
N_CHIP = N_Y * N_ZH
N_X, N_ZL = 4, 4
WEIGHT = 1e10
VMEM_LIMIT = 12 * 1024 * 1024


def dp_moves(dy=0, dz=0, dc=0):
    pairs = []
    for zh in range(N_ZH):
        for y in range(N_Y):
            for c in range(N_CORE):
                to = (((zh + dz) % N_ZH) * N_Y + (y + dy) % N_Y) * N_CORE + (c + dc) % N_CORE
                pairs.append(((zh * N_Y + y) * N_CORE + c, to))
    return pairs


def to_up(v):
    return lax.ppermute(v, "dp", dp_moves(dy=1))


def to_down(v):
    return lax.ppermute(v, "dp", dp_moves(dy=-1))


def to_far(v):
    return lax.ppermute(v, "dp", dp_moves(dz=1))


def to_core(v):
    return lax.ppermute(v, "dp", dp_moves(dc=1))


def swap_x(v, bit):
    return lax.ppermute(
        v, "replica", [(x * N_ZL + z, (x ^ bit) * N_ZL + z) for x in range(N_X) for z in range(N_ZL)]
    )


def swap_z(v, bit):
    return lax.ppermute(
        v, "replica", [(x * N_ZL + z, x * N_ZL + (z ^ bit)) for x in range(N_X) for z in range(N_ZL)]
    )


def core():
    return lax.rem(lax.axis_index("dp"), N_CORE)


def chip(side, dy):
    mine = lax.div(lax.axis_index("dp"), N_CORE)
    zh = lax.rem(lax.div(mine, N_Y) + side, N_ZH)
    return zh * N_Y + lax.rem(lax.rem(mine, N_Y) + dy, N_Y)


def place(side, dy):
    return chip(side, dy) * N_CORE + core()


def call(kernel, outs, ins, cost=1.0, vmem=VMEM_LIMIT, **kw):
    return pl.pallas_call(
        kernel,
        out_shape=outs,
        compiler_params=pltpu.CompilerParams(vmem_limit_bytes=vmem),
        cost_estimate=pl.CostEstimate(
            flops=int(cost * WEIGHT), bytes_accessed=0, transcendentals=0
        ),
        **kw,
    )(*ins)


HBM = pl.BlockSpec(memory_space=pltpu.HBM)
INSIDE = pl.BlockSpec(memory_space=pltpu.VMEM)


def full(shape):
    return pl.BlockSpec(shape, lambda j: (0,) * len(shape))


def block(index, size):
    return pl.ds(pl.multiple_of(index * size, size), size)


def dot_nt(a, b):
    return lax.dot_general(a, b, (((1,), (1,)), ((), ())), preferred_element_type=F32)


def dot(a, b):
    return jnp.dot(a, b, preferred_element_type=F32)


def identity(n):
    r = lax.broadcasted_iota(jnp.int32, (n, n), 0)
    c = lax.broadcasted_iota(jnp.int32, (n, n), 1)
    return jnp.where(r == c, 1.0, 0.0).astype(BF16)


def start_all(copies):
    for copy in copies:
        copy.start()
    return copies


ORDER = (2, 3, 1, 0)


def split_tokens(tokens, cot):
    t, d = tokens.shape
    f = cot.shape[1]
    steps = d // (2 * f)

    def kernel(tok, ct, mine, sent, extra, ir_out, sems):
        arrivals = []
        for i in range(steps):
            cols = slice(i * f, (i + 1) * f)
            arrivals += start_all(
                [
                    pltpu.make_async_copy(
                        tok.at[:, block(2 * i + core(), f)], mine.at[:, cols], sems.at[0, i]
                    ),
                    pltpu.make_async_copy(
                        tok.at[:, block(2 * i + 1 - core(), f)], sent.at[:, cols], sems.at[1, i]
                    ),
                ]
            )
        acc = jnp.zeros((t, 128), F32)
        for i in range(steps):
            arrivals[2 * i].wait()
            arrivals[2 * i + 1].wait()
            for n in range(i * f, (i + 1) * f, 128):
                for part in (mine, sent):
                    v = part[:, n : n + 128].astype(F32)
                    acc += v * v
        mean = jnp.sum(acc, axis=1, keepdims=True) / d
        ir = lax.rsqrt(jnp.broadcast_to(mean, (t, 128)) + epsilon)
        ir_out[...] = ir
        lane = lax.broadcasted_iota(jnp.int32, (t, 128), 1)
        terms = exact_terms(ir, lane, 0)
        extra[:, :f] = ct[...]
        extra[:, f:] = terms.astype(BF16)

    return call(
        kernel,
        (
            jax.ShapeDtypeStruct((t, d // 2), BF16),
            jax.ShapeDtypeStruct((t, d // 2), BF16),
            jax.ShapeDtypeStruct((t, f + 128), BF16),
            jax.ShapeDtypeStruct((t, 128), F32),
        ),
        (tokens, cot),
        cost=3.2,
        vmem=56 * 1024 * 1024,
        in_specs=[HBM, INSIDE],
        out_specs=(INSIDE,) * 4,
        scratch_shapes=[pltpu.SemaphoreType.DMA((2, steps))],
    )


def exact_terms(column, lane, first):
    high = column.astype(BF16).astype(F32)
    middle = (column - high).astype(BF16).astype(F32)
    low = column - high - middle
    zero = jnp.zeros_like(column)
    terms = jnp.where(lane == first, high, jnp.where(lane == first + 1, middle, zero))
    return jnp.where(lane == first + 2, low, terms)


def from_terms(values, first):
    return sum(values[:, first + i : first + i + 1].astype(F32) for i in range(3))


def partner_scale(extra, f):
    return from_terms(extra, f)


def hidden_block(hid, cols, own, oth, gain, irr, ext, side, dy):
    t = own.shape[0]
    f = cols.stop - cols.start
    g = gain[:, block(place(side, dy), f)]
    at = block(chip(side, dy), f)
    hid[:t, cols] = (own[:, at].astype(F32) * irr[:, 0:1] * g).astype(BF16)
    hid[t:, cols] = (oth[:, at].astype(F32) * partner_scale(ext, f) * g).astype(BF16)


def partials(mine, gains, cot, ir, other, extra, side):
    t = mine.shape[0]
    f = k = cot.shape[1]

    def kernel(own, oth, gain, ct, irr, ext, *refs):
        outs, hid, cot_t = refs[:4], refs[4], refs[5]
        eye = identity(k)
        cot_t[:, :t] = dot_nt(eye, ct[...]).astype(BF16)
        cot_t[:, t:] = dot_nt(eye, ext[:, :k]).astype(BF16)
        for i in range(N_Y):
            cols = slice(i * f, (i + 1) * f)
            hidden_block(hid, cols, own, oth, gain, irr, ext, side, ORDER[i])
            outs[i][...] = dot(cot_t[...], hid[:, cols]).astype(BF16)

    shape = jax.ShapeDtypeStruct((k, f), BF16)
    hidden = [] if side else [jax.ShapeDtypeStruct((2 * t, N_Y * f), BF16)]
    scratch = [pltpu.VMEM((2 * t, N_Y * f), BF16)] if side else []
    return call(
        kernel,
        [shape] * 4 + hidden,
        (mine, other, gains, cot, ir, extra),
        cost=3.4,
        in_specs=[INSIDE] * 6,
        out_specs=[INSIDE] * (4 + len(hidden)),
        scratch_shapes=scratch + [pltpu.VMEM((k, 2 * t), BF16)],
    )


def side_sum(own, from_down, from_up):
    def kernel(o, a, b, out):
        out[...] = (o[...].astype(F32) + a[...].astype(F32) + b[...].astype(F32)).astype(BF16)

    return call(kernel, jax.ShapeDtypeStruct(own.shape, BF16), (own, from_down, from_up), cost=1.0)


def final_sum(own, from_down, from_up, far, weight, gains):
    k, f = own.shape

    def kernel(o, a, b, fr, w, gain, out, gain_out):
        eye = identity(k)
        weight_t = dot_nt(eye, w[...])
        total = (o[...].astype(F32) + a[...].astype(F32)) + (b[...].astype(F32) + fr[...].astype(F32))
        out[...] = dot_nt(eye, total.astype(BF16)).astype(BF16)
        sums = jnp.sum(total * weight_t, axis=0, keepdims=True)
        gain_out[...] = (sums / gain[:, block(lax.axis_index("dp"), f)]).astype(BF16)

    return call(
        kernel,
        (jax.ShapeDtypeStruct((f, k), BF16), jax.ShapeDtypeStruct((1, f), BF16)),
        (own, from_down, from_up, far, weight, gains),
        cost=2.9,
    )


def project_near(hidden, weights):
    f, k = weights[0].shape

    def kernel(hid, w0, w1, w2, w3, out):
        total = jnp.zeros(out.shape, F32)
        for i, w in enumerate((w0, w1, w2, w3)):
            total += dot(hid[:, i * f : (i + 1) * f], w[...])
        out[...] = total

    return call(
        kernel,
        jax.ShapeDtypeStruct((hidden.shape[0], k), F32),
        (hidden,) + tuple(weights),
        cost=2.5,
        in_specs=[INSIDE] * 5,
        out_specs=INSIDE,
    )


def project_far(mine, other, gains, ir, extra, cot, weights, before):
    f, k = weights[0].shape
    t = mine.shape[0]

    def kernel(own_x, oth, gain, irr, ext, ct, w0, w1, w2, w3, first, kept, sent, hid):
        total = first[...]
        for i, w in enumerate((w0, w1, w2, w3)):
            cols = slice(i * f, (i + 1) * f)
            hidden_block(hid, cols, own_x, oth, gain, irr, ext, 1, ORDER[i])
            total += dot(hid[:, cols], w[...])
        own = jnp.sum(total[:t] * ct[...].astype(F32), axis=1, keepdims=True)
        others = jnp.sum(total[t:] * ext[:, :k].astype(F32), axis=1, keepdims=True)
        lane = lax.broadcasted_iota(jnp.int32, (t, 128), 1)
        kept[:, :k] = total[:t]
        kept[:, k:] = jnp.where(lane == 0, own, others)
        sent[:, :k] = total[t:].astype(BF16)
        sent[:, k:] = (exact_terms(others, lane, 0) + exact_terms(own, lane, 3)).astype(BF16)

    return call(
        kernel,
        (
            jax.ShapeDtypeStruct((t, k + 128), F32),
            jax.ShapeDtypeStruct((t, k + 128), BF16),
        ),
        (mine, other, gains, ir, extra, cot) + tuple(weights) + (before,),
        cost=2.5,
        in_specs=[INSIDE] * 11,
        out_specs=(INSIDE,) * 2,
        scratch_shapes=[pltpu.VMEM((2 * t, N_Y * f), BF16)],
    )


def blocks_of_chip():
    return [(side, dy) for side in range(N_ZH) for dy in ORDER]


def token_gradient(x, ws, gain, ct, scale, mean, store):
    f = ws[0].shape[0]
    shift = scale * scale * mean
    for i, (side, dy) in enumerate(blocks_of_chip()):
        g = gain[:, block(place(side, dy), f)]
        grad = dot_nt(ct, ws[i][...])
        values = x[:, block(chip(side, dy), f)].astype(F32)
        store(i, (scale * (grad * g) - values * shift).astype(BF16))


def backward_other(other, extra, gains, mine, arrived, weights):
    t = other.shape[0]
    f = k = extra.shape[1] - 128
    d = gains.shape[1]

    def kernel(*refs):
        oth, gain, ext, mn, arr = refs[:5]
        ws = refs[5:13]
        out, keys, mean = refs[13:16]
        keys[...] = (mn[:, :k] + arr[:, :k].astype(F32)).astype(BF16)
        own = (mn[:, k : k + 1] + from_terms(arr, k)) / d
        others = (mn[:, k + 1 : k + 2] + from_terms(arr, k + 3)) / d
        mean[...] = jnp.broadcast_to(own, (t, 128))

        def store(i, values):
            out[:, i * f : (i + 1) * f] = values

        token_gradient(oth, ws, gain, ext[:, :k], partner_scale(ext, f), others, store)

    return call(
        kernel,
        (
            jax.ShapeDtypeStruct((t, d // 2), BF16),
            jax.ShapeDtypeStruct((t, k), BF16),
            jax.ShapeDtypeStruct((t, 128), F32),
        ),
        (other, gains, extra, mine, arrived) + tuple(weights),
        cost=5.5,
        in_specs=[INSIDE] * 13,
        out_specs=(INSIDE,) * 3,
    )


def backward_own(mine, gains, ir, cot, mean, weights):
    t = mine.shape[0]
    d = gains.shape[1]
    f = cot.shape[1]
    where = blocks_of_chip()

    def kernel(*refs):
        own, gain, irr, ct, mn = refs[:5]
        ws = refs[5:13]
        out, results, sems = refs[13:]
        leaving = []

        def store(i, values):
            results[i] = values
            to = out.at[:, block(place(*where[i]), f)]
            leaving.extend(start_all([pltpu.make_async_copy(results.at[i], to, sems.at[i])]))

        token_gradient(own, ws, gain, ct[...], irr[:, 0:1], mn[:, 0:1], store)
        for copy in leaving:
            copy.wait()

    return call(
        kernel,
        jax.ShapeDtypeStruct((t, d), BF16),
        (mine, gains, ir, cot, mean) + tuple(weights),
        cost=4.7,
        in_specs=[INSIDE] * 13,
        out_specs=HBM,
        scratch_shapes=[
            pltpu.VMEM((N_CHIP, t, f), BF16),
            pltpu.SemaphoreType.DMA((N_CHIP,)),
        ],
    )


def fill_in(token_grad, arrived):
    f = arrived.shape[1] // N_CHIP
    where = blocks_of_chip()

    def kernel(_, arr, out, sems):
        away = 1 - core()
        leaving = []
        for i in range(N_CHIP):
            to = out.at[:, block(chip(*where[i]) * N_CORE + away, f)]
            leaving += start_all(
                [pltpu.make_async_copy(arr.at[:, i * f : (i + 1) * f], to, sems.at[i])]
            )
        for copy in leaving:
            copy.wait()

    return call(
        kernel,
        jax.ShapeDtypeStruct(token_grad.shape, token_grad.dtype),
        (token_grad, arrived),
        cost=1.4,
        in_specs=[HBM, INSIDE],
        out_specs=HBM,
        input_output_aliases={0: 0},
        scratch_shapes=[pltpu.SemaphoreType.DMA((N_CHIP,))],
    )


def x_bit(bit):
    return lax.rem(lax.div(lax.axis_index("replica"), N_ZL * bit), 2)


def scaled_halves(quantized, exponents):
    n, cols = quantized.shape
    h = n // 2
    nb = exponents.shape[0]
    width = cols // nb

    def kernel(q, e, keep, send, scales):
        powers = jnp.exp2(e[...].astype(F32)).astype(BF16)
        scales[...] = dot_nt(identity(n), powers)
        for out, half in ((keep, x_bit(1)), (send, 1 - x_bit(1))):
            rows = block(half, h)
            for b in range(nb):
                lanes = slice(b * width, (b + 1) * width)
                scale = scales[rows, b : b + 1]
                out[:, lanes] = (q[rows, lanes].astype(F32) * scale).astype(BF16)

    return call(
        kernel,
        (jax.ShapeDtypeStruct((h, cols), BF16),) * 2,
        (quantized, exponents),
        cost=2.5,
        scratch_shapes=[pltpu.VMEM((n, nb), F32)],
    )


def outer_update(average, momentum, outer_params):
    new_momentum = outer_decay * momentum + average
    new_params = outer_params - outer_rate * (average + outer_decay * new_momentum)
    return (new_momentum, new_params)


def outer_step(half, other, momentum, outer_params):
    n, cols = momentum.shape
    h = n // 2

    def kernel(a, b, m, p, new_m, new_p):
        j = pl.program_id(0)

        def update(total):
            average = total[...].astype(F32) / (N_X * N_ZL)
            new_m[...], new_p[...] = outer_update(average, m[...], p[...])

        pl.when(j == 0)(lambda: update(a))
        pl.when(j == 1)(lambda: update(b))

    def half_of(j):
        return (lax.rem(x_bit(1) + j, 2), 0)

    spec = pl.BlockSpec((h, cols), half_of)
    return call(
        kernel,
        (jax.ShapeDtypeStruct((n, cols), F32),) * 2,
        (half, other, momentum, outer_params),
        cost=2.0,
        grid=(2,),
        in_specs=[full((h, cols)), full((h, cols)), spec, spec],
        out_specs=(spec, spec),
    )


def after(values, *events):
    held = lax.optimization_barrier(tuple(values) + events)
    return held[: len(values)]


def shards(
    tokens, norm_gain, key_weight, key_cotangent, quantized, scale_exponent, momentum, outer_params
):
    gains = norm_gain
    cot = key_cotangent
    weight = key_weight[0]

    n_down = to_up(weight)
    n_up = to_down(weight)

    mine, sent, extra_sent, ir = split_tokens(tokens, cot)
    other = to_core(sent)
    extra = to_core(extra_sent)

    quant, exponents = after((quantized[0], scale_exponent[0]), ir)
    keep, send = scaled_halves(quant, exponents.T)
    x1 = swap_x(send, 1)
    far_weight = to_far(after((weight,), keep)[0])

    other, extra = after((other, extra), keep)
    f_opposite, f_minus, f_plus, f_own = partials(
        mine, gains, cot, ir, other, extra, 1
    )
    n_down, n_up = after((n_down, n_up), f_own)
    n_opposite = to_up(n_down)
    f_step = to_down(f_opposite)
    f_from_down = to_up(f_plus)

    keep, x1 = after((keep, x1), n_up)
    part = keep + x1
    x2 = swap_x(part, 2)

    other, extra = after((other, extra), part)
    g_opposite, g_minus, g_plus, g_own, hidden_near = partials(
        mine, gains, cot, ir, other, extra, 0
    )
    part, x2 = after((part, x2), g_own)
    part = part + x2
    z1 = swap_z(part, 1)

    f_minus, f_step = after((f_minus, f_step), part)
    f_minus = f_minus + f_step
    f_from_up = to_down(f_minus)

    near_rows = (n_opposite, n_down, n_up, weight)
    *near_rows, hidden_near = after((*near_rows, hidden_near), f_minus)
    near_keys = project_near(hidden_near, near_rows)

    (far_weight,) = after((far_weight,), near_keys)
    a_down = to_up(far_weight)
    a_up = to_down(far_weight)
    part, z1 = after((part, z1), far_weight)
    part = part + z1
    z2 = swap_z(part, 2)

    f_own, f_from_down, f_from_up = after((f_own, f_from_down, f_from_up), part)
    f_total = side_sum(f_own, f_from_down, f_from_up)
    far_sum = to_far(f_total)
    part, z2 = after((part, z2), f_total)
    part = part + z2
    x3 = swap_x(part, 1)
    (a_down,) = after((a_down,), part)
    a_opposite = to_up(a_down)

    g_opposite, a_up = after((g_opposite, a_up), a_down)
    g_step = to_down(g_opposite)
    g_plus, a_opposite = after((g_plus, a_opposite), a_up)
    g_from_down = to_up(g_plus)

    far_rows = (a_opposite, a_down, a_up, far_weight)
    keys_mine, keys_sent = project_far(
        mine, other, gains, ir, extra, cot, far_rows, near_keys
    )
    arrived = to_core(keys_sent)
    part, x3 = after((part, x3), keys_sent)
    new_momentum, new_params = outer_step(part, x3, momentum, outer_params)
    g_minus, g_step = after((g_minus, g_step), new_params)
    g_minus = g_minus + g_step
    g_from_up = to_down(g_minus)
    arrived, keys_mine, far_sum = after((arrived, keys_mine, far_sum), g_minus)
    rows = tuple(near_rows) + tuple(far_rows)
    grad_sent, keys, mean = backward_other(other, extra, gains, keys_mine, arrived, rows)
    grad_arrived = to_core(grad_sent)
    mean, far_sum = after((mean, far_sum), grad_sent)
    token_grad = backward_own(mine, gains, ir, cot, mean, rows)
    grad_arrived, token_grad = after((grad_arrived, token_grad), new_params)
    token_grad = fill_in(token_grad, grad_arrived)
    (g_from_up,) = after((g_from_up,), token_grad)
    weight_grad, gain_grad = final_sum(g_own, g_from_down, g_from_up, far_sum, weight, gains)
    return (keys, token_grad, weight_grad[None], gain_grad, new_momentum, new_params)


def solution(mesh):
    return jax.shard_map(
        shards,
        mesh=mesh,
        in_specs=(
            P(("replica", "dp"), None),
            P("replica", None),
            P("replica", "dp", None),
            P(("replica", "dp"), None),
            P("replica", "dp", None),
            P("replica", "dp", None),
            P("dp", None),
            P("dp", None),
        ),
        out_specs=(
            P(("replica", "dp"), None),
            P(("replica", "dp"), None),
            P("replica", "dp", None),
            P("replica", "dp"),
            P("dp", None),
            P("dp", None),
        ),
        check_vma=False,
    )
```
